32 devices in a mesh: dp: 8 (over z, x), pipe: 4 (over y, core).
Axes of the slice: x: 2, y: 2, z: 4, core: 2. Of those that a mesh axis runs over, the one named last changes fastest.
Arguments:
- inputs: bfloat16 [24, 256, 768], P('dp', 'pipe'), may hold values from -6 to 6
- lengths: int32 [24], P('dp'), may hold values from 32 to 256, as said below
- w_qkv: bfloat16 [768, 2304], replicated, may hold values from -0.21875 to 0.21875
- w_out: bfloat16 [768, 768], replicated, may hold values from -0.875 to 0.875
- w_up: bfloat16 [768, 3072], replicated, may hold values from -0.21875 to 0.21875
- w_down: bfloat16 [3072, 768], replicated, may hold values from -0.109375 to 0.109375
- norm1_gain: float32 [768], replicated, may hold values from 0.1 to 1.9
- norm1_shift: float32 [768], replicated, may hold values from -3 to 3
- norm2_gain: float32 [768], replicated, may hold values from 0.1 to 1.9
- norm2_shift: float32 [768], replicated, may hold values from -3 to 3
- pass_embed: float32 [768], replicated, may hold values from -3 to 3
- cotangent: bfloat16 [24, 256, 768], P('dp', 'pipe'), may hold values from -6 to 6
Outputs:
- block_out: bfloat16 [24, 256, 768], P('dp', 'pipe')
- input_grads: bfloat16 [24, 256, 768], P('dp', 'pipe')
- grad_qkv: float32 [768, 2304], P('pipe')
- grad_out: float32 [768, 768], P('pipe')
- grad_up: float32 [768, 3072], P('pipe')
- grad_down: float32 [3072, 768], P('pipe')
- grad_norm1_gain: float32 [768], P('pipe')
- grad_norm1_shift: float32 [768], P('pipe')
- grad_norm2_gain: float32 [768], P('pipe')
- grad_norm2_shift: float32 [768], P('pipe')
- grad_pass_embed: float32 [768], P('pipe')
The draws below stay inside these ranges and needn't reach their ends.
Inputs may be any that keep to these rules, and one draw needn't show every extreme that they name: `lengths`: in each aligned group of 3 sequences, one has length 256.
All inputs are finite; a program needn't handle non-finite values.
Results may differ from the reference program's by a relative error of at most 0.018.
Values may be sent and summed in bfloat16 or wider, within the bound.
A program may use at most 320 MiB of HBM per device.

```python
import jax
import jax.numpy as jnp
from jax import lax

D = 768
HEADS = 12
HEAD = 64
FF = 3072
SEQ = 256
MICRO = 3
SEQS = 24


def draw_lengths(key, part):
    key = jax.random.fold_in(key, 7)
    first_key, second_key = jax.random.split(key)
    base = jax.random.randint(first_key, (SEQS,), SEQ // 8, SEQ + 1)
    chosen = jax.random.randint(second_key, (SEQS // MICRO,), 0, MICRO)
    place = jnp.arange(SEQS) % MICRO
    full = place == jnp.repeat(chosen, MICRO)
    return jnp.where(full, SEQ, base).astype(jnp.int32)


def level_of(rng, shape, cuts, low, top_value):
    level = 1.0
    for position, blocks in cuts:
        draws = jax.random.uniform(jax.random.fold_in(jax.random.fold_in(rng, 6), position), (blocks,), jnp.float32, low / len(cuts), top_value / len(cuts))
        level = level * jnp.repeat(jnp.exp(draws), shape[position] // blocks).reshape((-1,) + (1,) * (len(shape) - 1 - position))
    return level


def gaussian(stream_key, shape, width, most, shards=(), dtype=jnp.bfloat16):
    values = jax.random.normal(stream_key, shape, jnp.float32) * width
    if len(shards) > 0:
        values = level_of(stream_key, shape, shards, -0.22, 0.18) * values
    return jnp.clip(values, min=-most, max=most).astype(dtype)


def setup_inputs(seed: int = 0) -> dict:
    arg_keys = jax.random.split(jax.random.key(seed), 13)
    return {
        "inputs": gaussian(arg_keys[0], (SEQS, SEQ, D), 1.0, 6.0, ((0, 8), (1, 4))),
        "lengths": draw_lengths(jax.random.fold_in(arg_keys[12], 71), 0),
        "w_qkv": gaussian(arg_keys[2], (D, 3 * D), D ** -0.5, 0.21875),
        "w_out": gaussian(arg_keys[3], (D, D), (D // 16) ** -0.5, 0.875),
        "w_up": gaussian(arg_keys[4], (D, FF), D ** -0.5, 0.21875),
        "w_down": gaussian(arg_keys[5], (FF, D), FF ** -0.5, 0.109375),
        "norm1_gain": jnp.clip(1.0 + 0.18 * jax.random.normal(arg_keys[6], (D,), jnp.float32), 0.1, 1.9),
        "norm1_shift": gaussian(arg_keys[7], (D,), 0.5, 3.0, (), jnp.float32),
        "norm2_gain": jnp.clip(1.0 + 0.18 * jax.random.normal(arg_keys[8], (D,), jnp.float32), 0.1, 1.9),
        "norm2_shift": gaussian(arg_keys[9], (D,), 0.5, 3.0, (), jnp.float32),
        "pass_embed": gaussian(arg_keys[10], (D,), 0.5, 3.0, (), jnp.float32),
        "cotangent": gaussian(arg_keys[11], (SEQS, SEQ, D), 1.0, 6.0, ((0, 8), (1, 4))),
    }


@jax.custom_vjp
def low(v):
    return lax.optimization_barrier(v.astype(jnp.bfloat16)).astype(jnp.float32)

@jax.custom_vjp
def low_back(v):
    return v

def low_keep(v):
    return (low(v), None)

def low_pass(kept, grad):
    return (grad,)

def back_keep(v):
    return (v, None)

def back_low(kept, grad):
    return (low(grad),)
low.defvjp(low_keep, low_pass)
low_back.defvjp(back_keep, back_low)
HIGH = lax.Precision.HIGHEST

def normalize(values, gain, shift):
    center = values - lax.optimization_barrier(jnp.mean(values, axis=-1, keepdims=True))
    spread = lax.optimization_barrier(jnp.mean(center * center, axis=-1, keepdims=True))
    return center * lax.rsqrt(spread + 1e-05) * gain + shift

def product(left, right):
    return jnp.dot(left, right, precision=HIGH)

def attention(queries, key_rows, value_rows, allowed):
    row_count = queries.shape[0]
    q_heads = queries.reshape(row_count, HEADS, HEAD)
    k_heads = key_rows.reshape(key_rows.shape[0], HEADS, HEAD)
    v_heads = value_rows.reshape(value_rows.shape[0], HEADS, HEAD)
    scores = low_back(jnp.einsum('qhd,khd->hqk', q_heads, k_heads, precision=HIGH) * HEAD ** (-0.5))
    scores = jnp.where(allowed[None], scores, -1e+30)
    row_max = lax.optimization_barrier(jnp.max(scores, axis=-1, keepdims=True))
    weights = jnp.exp(scores - row_max)
    soft = low(weights / lax.optimization_barrier(jnp.sum(weights, axis=-1, keepdims=True)))
    context = jnp.einsum('hqk,khd->qhd', soft, v_heads, precision=HIGH)
    return low_back(low(context.reshape(row_count, HEADS * HEAD)))

def block(state, params, extra, allowed):
    w_qkv, w_out, w_up, w_down, gain_one, shift_one, gain_two, shift_two = params
    features = state.shape[1]
    normed = low(normalize(state, gain_one, shift_one))
    qkv = low_back(low(product(normed, w_qkv)))
    queries = qkv[:, :features]
    key_new = qkv[:, features:2 * features]
    value_new = qkv[:, 2 * features:]
    if extra is None:
        key_rows, value_rows = (key_new, value_new)
    else:
        key_rows = jnp.concatenate([extra[0], key_new], axis=0)
        value_rows = jnp.concatenate([extra[1], value_new], axis=0)
    residual = state + low_back(product(attention(queries, key_rows, value_rows, allowed), w_out))
    normed_two = low(normalize(residual, gain_two, shift_two))
    hidden = low_back(product(normed_two, w_up))
    active = low(jax.nn.gelu(hidden, approximate=True))
    return (residual + low_back(product(active, w_down)), key_new, value_new)

def sequence(state, params, pass_embed, length):
    places = jnp.arange(SEQ)
    inside = places < length
    causal = (places[None, :] <= places[:, None]) & inside[None, :]
    first, key_first, value_first = block(state, params, None, causal)
    second_in = low_back(low(first)) + pass_embed
    second, key_unused, value_unused = block(second_in, params, (key_first, value_first), jnp.concatenate([causal, causal], axis=1))
    return second * inside[:, None].astype(jnp.float32)

def reference(inputs, lengths, w_qkv, w_out, w_up, w_down, norm1_gain, norm1_shift, norm2_gain, norm2_shift, pass_embed, cotangent):
    params = tuple((array.astype(jnp.float32) for array in (w_qkv, w_out, w_up, w_down, norm1_gain, norm1_shift, norm2_gain, norm2_shift)))
    embed = pass_embed.astype(jnp.float32)

    def one_sequence(totals, item):
        state, length, grad_seq = item

        def run(state_in, params_in, embed_in):
            return sequence(state_in, params_in, embed_in, length)
        result, pull = jax.vjp(run, state.astype(jnp.float32), params, embed)
        d_state, d_params, d_embed = pull(grad_seq.astype(jnp.float32))
        totals = jax.tree.map(lambda old, new: old + new, totals, (d_params, d_embed))
        return (totals, (result.astype(jnp.bfloat16), d_state.astype(jnp.bfloat16)))
    zeros = jax.tree.map(jnp.zeros_like, (params, embed))
    totals, (block_out, input_grads) = lax.scan(one_sequence, zeros, (inputs, lengths, cotangent))
    grads, grad_embed = totals
    return (block_out, input_grads, grads[0], grads[1], grads[2], grads[3], grads[4], grads[5], grads[6], grads[7], grad_embed)
```

```python
import functools

import jax
import jax.numpy as jnp
from jax import lax
from jax.experimental import pallas as pl
from jax.experimental.pallas import tpu as pltpu
from jax.sharding import PartitionSpec as P

MESH = pl.DeviceIdType.MESH
HEADS = 12
HEAD = 64
F32 = jnp.float32
BF16 = jnp.bfloat16
ANY = pl.BlockSpec(memory_space=pl.ANY)
VMEM = pl.BlockSpec(memory_space=pltpu.VMEM)
SMEM = pl.BlockSpec(memory_space=pltpu.SMEM)


def dot(left, right):
    return jnp.dot(left, right, preferred_element_type=F32)


def dot_nt(left, right):
    return lax.dot_general(left, right, (((1,), (1,)), ((), ())), preferred_element_type=F32)


def normalize(values):
    center = values - jnp.mean(values, axis=-1, keepdims=True)
    scale = lax.rsqrt(jnp.mean(center * center, axis=-1, keepdims=True) + 1e-05)
    return center * scale, scale


def chain_kernel(
    x_ref, cot_ref, len_ref, gain1_ref, shift1_ref, gain2_ref, shift2_ref, embed_ref,
    wqkv_hbm, wout_hbm, wup_hbm, wdown_hbm,
    left_hbm, right_hbm, out_ref, grad_ref, vec_ref,
    wqkv, wout, wup, wdown, left, right, qkv, vt, kt, lse, gp, mixed, state, ctx,
    dk_more, dv_more, dqt, dctx, bias, w_sem, o_sem,
):
    seq, feat = x_ref.shape
    ff = wup.shape[1]
    tiles = ff // feat
    half = feat // 6
    weight_copies = [
        pltpu.make_async_copy(src, dst, w_sem.at[i])
        for i, (src, dst) in enumerate(
            ((wqkv_hbm, wqkv), (wout_hbm, wout), (wup_hbm, wup), (wdown_hbm, wdown))
        )
    ]
    for copy in weight_copies:
        copy.start()

    length = len_ref[0]
    keys = lax.broadcasted_iota(jnp.int32, (seq, seq), 0)
    queries = lax.broadcasted_iota(jnp.int32, (seq, seq), 1)
    bias[...] = jnp.where((keys <= queries) & (keys < length), 0.0, -1e30).astype(F32)
    inside = (lax.broadcasted_iota(jnp.int32, (seq, 1), 0) < length).astype(F32)
    low_lanes = lax.broadcasted_iota(jnp.int32, (seq, half), 1) < HEAD

    def pick(values, head):
        zero = jnp.zeros_like(values)
        return jnp.where(low_lanes, values, zero) if head == 0 else jnp.where(low_lanes, zero, values)

    def rows_of(i):
        return pl.ds(i * seq, seq)

    def put_left(offset, i, values):
        left[pl.ds(offset, values.shape[1]), rows_of(i)] = values.T

    N2, CTX, N1 = ff, ff + feat, ff + 2 * feat
    HID, ATT, QKV = feat, feat + ff, 2 * feat + ff

    def forward(i):
        value = state[i]
        n1 = (normalize(value)[0] * gain1_ref[...] + shift1_ref[...]).astype(BF16)
        put_left(N1, i, n1)
        if i == 0:
            weight_copies[0].wait()
        for j in range(3):
            part = dot(n1, wqkv[:, j * feat : (j + 1) * feat])
            if j == 0:
                part = part * HEAD ** (-0.5)
            part = part.astype(BF16)
            qkv[i, :, j * feat : (j + 1) * feat] = part
            if j == 1:
                kt[i] = part.T
            if j == 2:
                vt[i] = part.T

        def pair(hp, carry):
            lanes = pl.ds(pl.multiple_of(hp * half, half), half)
            q2 = qkv[i, :, lanes]
            for head in range(2):
                qm = pick(q2, head)
                scores = []
                for b in range(i + 1):
                    k2 = qkv[b, :, pl.ds(pl.multiple_of(feat + hp * half, half), half)]
                    scores.append(dot_nt(k2, qm) + bias[...])
                top = jnp.max(scores[0], axis=0, keepdims=True)
                for s in scores[1:]:
                    top = jnp.maximum(top, jnp.max(s, axis=0, keepdims=True))
                weights = [jnp.exp(s - top) for s in scores]
                total = jnp.sum(weights[0], axis=0, keepdims=True)
                for w in weights[1:]:
                    total = total + jnp.sum(w, axis=0, keepdims=True)
                inv = 1.0 / total
                lse[i, pl.ds(2 * hp + head, 1), :] = top + jnp.log(total)
                rows = pl.ds(pl.multiple_of(hp * half + head * HEAD, HEAD), HEAD)
                acc = None
                for b in range(i + 1):
                    term = dot(vt[b, rows, :], (weights[b] * inv).astype(BF16))
                    acc = term if acc is None else acc + term
                left[pl.ds(pl.multiple_of(CTX + hp * half + head * HEAD, HEAD), HEAD), rows_of(i)] = acc.astype(BF16)
            return carry

        lax.fori_loop(0, feat // half, pair, 0)
        ctx[...] = left[pl.ds(CTX, feat), rows_of(i)].T
        if i == 0:
            weight_copies[1].wait()
        mix = state[i] + dot(ctx[...], wout[...])
        mixed[i] = mix
        n2 = (normalize(mix)[0] * gain2_ref[...] + shift2_ref[...]).astype(BF16)
        put_left(N2, i, n2)
        if i == 0:
            weight_copies[2].wait()
            weight_copies[3].wait()
        acc = mix
        for j in range(tiles):
            u = dot(n2, wup[:, j * feat : (j + 1) * feat])
            c = 0.7978845608028654
            square = u * u
            th = jnp.tanh(c * u * (1.0 + 0.044715 * square))
            halfp = 0.5 + 0.5 * th
            active = (u * halfp).astype(BF16)
            slope = halfp + 0.5 * u * (1.0 - th * th) * (c * (1.0 + 3 * 0.044715 * square))
            gp[i, :, j * feat : (j + 1) * feat] = slope.astype(BF16)
            put_left(j * feat, i, active)
            acc = acc + dot(active, wdown[j * feat : (j + 1) * feat, :])
        return acc

    def norm_back(values, d_out, gain, slot, first):
        norm, scale = normalize(values)
        g_gain = jnp.sum(d_out * norm, axis=0, keepdims=True)
        g_shift = jnp.sum(d_out, axis=0, keepdims=True)
        if first:
            vec_ref[slot : slot + 1, :] = g_gain
            vec_ref[slot + 1 : slot + 2, :] = g_shift
        else:
            vec_ref[slot : slot + 1, :] += g_gain
            vec_ref[slot + 1 : slot + 2, :] += g_shift
        t = d_out * gain
        return scale * (t - jnp.mean(t, axis=-1, keepdims=True) - norm * jnp.mean(t * norm, axis=-1, keepdims=True))

    def backward(i, grad):
        branch = grad.astype(BF16)
        right[rows_of(i), 0:feat] = branch
        acc = None
        for j in range(tiles):
            d_active = dot_nt(branch, wdown[j * feat : (j + 1) * feat, :])
            d_hidden = (d_active * gp[i, :, j * feat : (j + 1) * feat].astype(F32)).astype(BF16)
            right[rows_of(i), HID + j * feat : HID + (j + 1) * feat] = d_hidden
            term = dot_nt(d_hidden, wup[:, j * feat : (j + 1) * feat])
            acc = term if acc is None else acc + term
        d_mixed = grad + norm_back(mixed[i], acc, gain2_ref[...], 2, i == 1)
        d_attn = d_mixed.astype(BF16)
        right[rows_of(i), ATT : ATT + feat] = d_attn
        dctx[...] = dot_nt(d_attn, wout[...]).astype(BF16)

        def pair(hp, carry):
            lanes = pl.ds(pl.multiple_of(hp * half, half), half)
            q2 = qkv[i, :, lanes]
            do2 = dctx[:, lanes]
            dk = [None] * (i + 1)
            dv = [None] * (i + 1)
            for head in range(2):
                qm = pick(q2, head)
                dom = pick(do2, head)
                row = lse[i, pl.ds(2 * hp + head, 1), :]
                soft, d_soft = [], []
                inner = None
                for b in range(i + 1):
                    k2 = qkv[b, :, pl.ds(pl.multiple_of(feat + hp * half, half), half)]
                    v2 = qkv[b, :, pl.ds(pl.multiple_of(2 * feat + hp * half, half), half)]
                    soft.append(jnp.exp(dot_nt(k2, qm) + (bias[...] - row)))
                    d_soft.append(dot_nt(v2, dom))
                    term = jnp.sum(soft[b] * d_soft[b], axis=0, keepdims=True)
                    inner = term if inner is None else inner + term
                rows = pl.ds(pl.multiple_of(hp * half + head * HEAD, HEAD), HEAD)
                dq = None
                for b in range(i + 1):
                    d_score = (soft[b] * (d_soft[b] - inner)).astype(BF16)
                    term_v = dot(soft[b].astype(BF16), dom)
                    term_k = dot(d_score, qm)
                    term_q = dot(kt[b, rows, :], d_score)
                    dv[b] = term_v if dv[b] is None else dv[b] + term_v
                    dk[b] = term_k if dk[b] is None else dk[b] + term_k
                    dq = term_q if dq is None else dq + term_q
                dqt[rows, :] = (dq * HEAD ** (-0.5)).astype(BF16)
            dk_own, dv_own = dk[i], dv[i]
            if i == 1:
                dk_more[:, lanes] = dk[0]
                dv_more[:, lanes] = dv[0]
            else:
                dk_own = dk_own + dk_more[:, lanes]
                dv_own = dv_own + dv_more[:, lanes]
            right[rows_of(i), pl.ds(pl.multiple_of(QKV + feat + hp * half, half), half)] = dk_own.astype(BF16)
            right[rows_of(i), pl.ds(pl.multiple_of(QKV + 2 * feat + hp * half, half), half)] = dv_own.astype(BF16)
            return carry

        lax.fori_loop(0, feat // half, pair, 0)
        right[rows_of(i), QKV : QKV + feat] = dqt[...].T
        d_normed = None
        for j in range(3):
            term = dot_nt(
                right[rows_of(i), QKV + j * feat : QKV + (j + 1) * feat], wqkv[:, j * feat : (j + 1) * feat]
            )
            d_normed = term if d_normed is None else d_normed + term
        return d_mixed + norm_back(state[i], d_normed, gain1_ref[...], 0, i == 1)

    state[0] = x_ref[...].astype(F32)
    first = forward(0)
    state[1] = first.astype(BF16).astype(F32) + embed_ref[...]
    second = forward(1)
    out_ref[...] = (second * inside).astype(BF16)
    left_copy = pltpu.make_async_copy(left, left_hbm, o_sem.at[0])
    left_copy.start()
    d_carry = backward(1, cot_ref[...].astype(F32) * inside)
    vec_ref[4:5, :] = jnp.sum(d_carry, axis=0, keepdims=True)
    vec_ref[5:8, :] = jnp.zeros((3, feat), F32)
    d_state = backward(0, d_carry.astype(BF16).astype(F32))
    grad_ref[...] = d_state.astype(BF16)
    right_copy = pltpu.make_async_copy(right, right_hbm, o_sem.at[1])
    right_copy.start()
    left_copy.wait()
    right_copy.wait()


def run_chain(x, cot, length, gain1, shift1, gain2, shift2, embed, w_qkv, w_out, w_up, w_down):
    seq, feat = x.shape
    ff = w_up.shape[1]
    rows = [v.reshape(1, feat) for v in (gain1, shift1, gain2, shift2, embed)]
    left_rows = ff + 3 * feat
    right_cols = 5 * feat + ff
    return pl.pallas_call(
        chain_kernel,
        out_shape=(
            jax.ShapeDtypeStruct((left_rows, 2 * seq), BF16),
            jax.ShapeDtypeStruct((2 * seq, right_cols), BF16),
            jax.ShapeDtypeStruct((seq, feat), BF16),
            jax.ShapeDtypeStruct((seq, feat), BF16),
            jax.ShapeDtypeStruct((8, feat), F32),
        ),
        in_specs=[VMEM, VMEM, SMEM] + [VMEM] * 5 + [ANY] * 4,
        out_specs=(ANY, ANY, VMEM, VMEM, VMEM),
        scratch_shapes=[
            pltpu.VMEM(w_qkv.shape, BF16),
            pltpu.VMEM(w_out.shape, BF16),
            pltpu.VMEM(w_up.shape, BF16),
            pltpu.VMEM(w_down.shape, BF16),
            pltpu.VMEM((left_rows, 2 * seq), BF16),
            pltpu.VMEM((2 * seq, right_cols), BF16),
            pltpu.VMEM((2, seq, 3 * feat), BF16),
            pltpu.VMEM((2, feat, seq), BF16),
            pltpu.VMEM((2, feat, seq), BF16),
            pltpu.VMEM((2, 16, seq), F32),
            pltpu.VMEM((2, seq, ff), BF16),
            pltpu.VMEM((2, seq, feat), F32),
            pltpu.VMEM((2, seq, feat), F32),
            pltpu.VMEM((seq, feat), BF16),
            pltpu.VMEM((seq, feat), F32),
            pltpu.VMEM((seq, feat), F32),
            pltpu.VMEM((feat, seq), BF16),
            pltpu.VMEM((seq, feat), BF16),
            pltpu.VMEM((seq, seq), F32),
            pltpu.SemaphoreType.DMA((4,)),
            pltpu.SemaphoreType.DMA((2,)),
        ],
        compiler_params=pltpu.CompilerParams(vmem_limit_bytes=58 * 2**20),
    )(x, cot, length, *rows, w_qkv, w_out, w_up, w_down)


def exchange_kernel(in_ref, cot_ref, x_ref, c_ref, x_send, x_recv, c_send, c_recv, local):
    g = lax.axis_index("dp")
    p = lax.axis_index("pipe")
    slots, block, feat = in_ref.shape
    size = slots + 1
    barrier = pltpu.get_barrier_semaphore()
    for j in range(1, size):
        pl.semaphore_signal(barrier, inc=1, device_id=(g, (p + j) % size), device_id_type=MESH)
    pl.semaphore_wait(barrier, size - 1)
    mine = pl.ds(pl.multiple_of(p * block, block), block)

    def copies(j):
        peer = (p + j) % size
        slot = jnp.maximum(peer - 1, 0)
        return [
            pltpu.make_async_remote_copy(
                src.at[slot], dst.at[mine], send.at[j - 1], recv.at[j - 1],
                device_id=(g, peer), device_id_type=MESH,
            )
            for src, dst, send, recv in ((in_ref, x_ref, x_send, x_recv), (cot_ref, c_ref, c_send, c_recv))
        ]

    for j in range(1, size):
        @pl.when((p + j) % size > 0)
        def _(j=j):
            for copy in copies(j):
                copy.start()

    @pl.when(p > 0)
    def _():
        own = [
            pltpu.make_async_copy(in_ref.at[p - 1], x_ref.at[mine], local.at[0]),
            pltpu.make_async_copy(cot_ref.at[p - 1], c_ref.at[mine], local.at[1]),
        ]
        for copy in own:
            copy.start()
        for copy in own:
            copy.wait()
        for j in range(1, size):
            for copy in copies(j):
                copy.wait_recv()

    @pl.when(p == 0)
    def _():
        x_ref[...] = jnp.zeros(x_ref.shape, x_ref.dtype)
        c_ref[...] = jnp.zeros(c_ref.shape, c_ref.dtype)

    for j in range(1, size):
        @pl.when((p + j) % size > 0)
        def _(j=j):
            for copy in copies(j):
                copy.wait_send()


def run_exchange(inputs, cotangent):
    slots, block, feat = inputs.shape
    size = slots + 1
    whole = jax.ShapeDtypeStruct((size * block, feat), BF16)
    return pl.pallas_call(
        exchange_kernel,
        out_shape=(whole, whole),
        in_specs=[VMEM, VMEM],
        out_specs=(VMEM, VMEM),
        scratch_shapes=[pltpu.SemaphoreType.DMA((size - 1,))] * 4 + [pltpu.SemaphoreType.DMA((2,))],
        compiler_params=pltpu.CompilerParams(collective_id=0, has_side_effects=True),
    )(inputs, cotangent)


ZED = 4


def reduce_kernel(
    dims, left_hbm, right_hbm, out_seq, grad_seq, vec_in,
    sums_hbm, out_ref, gin_ref, vec_ref,
    left, right, own, give, d_recv, y_send, y_keep, y_recv, x_send, x_keep, x_recv,
    z_send, z_recv, w_send, w_recv, full, vec_recv,
    l_sem, r_sem, d_ss, d_rs, y_ss, y_rs, x_ss, x_rs, z_ss, z_rs, w_ss, w_rs, g_ss, g_rs, h_ss, h_rs, s_sem,
    o_ss, o_rs, v_ss, v_rs, local,
):
    feat, ff, rows, lags, groups = dims
    units = (2 * ff + 4 * feat) // feat
    quarter = feat // 4
    subs = quarter // rows
    chunks = units * subs
    tiles = ff // feat
    piece = rows // ZED
    g = lax.axis_index("dp")
    p = lax.axis_index("pipe")
    core, y = p % 2, p // 2
    x, z, w = g % 2, (g // 2) % ZED, g // (2 * ZED)
    sib = (g, p + 1 - 2 * core)
    ypeer = (g, p + 2 - 4 * y)
    diag = (g, 3 - p)
    xpeer = (g + 1 - 2 * x, p)

    def zpeer(j):
        return (g + 2 * ((z + j) % ZED - z), p)

    def wpeer(j):
        return (g + 2 * ZED * ((w + j) % groups - w), p)

    everyone = [sib, ypeer, diag, xpeer] + [zpeer(j) for j in range(1, ZED)] + [wpeer(j) for j in range(1, groups)]

    loads_r = [
        pltpu.make_async_copy(
            right_hbm.at[:, pl.ds(u * feat, feat)], right.at[:, pl.ds(u * feat, feat)], r_sem.at[u]
        )
        for u in range(units - tiles + 1)
    ]
    starts = (0, ff, ff + feat, ff + 2 * feat, ff + 3 * feat)
    loads_l = [
        pltpu.make_async_copy(left_hbm.at[pl.ds(a, b - a)], left.at[pl.ds(a, b - a)], l_sem.at[i])
        for i, (a, b) in enumerate(zip(starts[:-1], starts[1:]))
    ]
    loads_r[0].start()
    loads_l[0].start()
    loads_l[1].start()
    for copy in loads_r[1:]:
        copy.start()
    loads_l[2].start()
    loads_l[3].start()

    barrier = pltpu.get_barrier_semaphore()
    for device in everyone:
        pl.semaphore_signal(barrier, inc=1, device_id=device, device_id_type=MESH)
    pl.semaphore_wait(barrier, len(everyone))

    slots, block, _ = out_ref.shape
    size = slots + 1

    def result_copies(j):
        peer = (p + j) % size
        slot = jnp.maximum(p - 1, 0)
        part = pl.ds(pl.multiple_of(peer * block, block), block)
        return [
            pltpu.make_async_remote_copy(
                src.at[part], dst.at[slot], o_ss.at[n, j - 1], o_rs.at[n, j - 1],
                device_id=(g, peer), device_id_type=MESH,
            )
            for n, (src, dst) in enumerate(((out_seq, out_ref), (grad_seq, gin_ref)))
        ]

    def own_results():
        part = pl.ds(pl.multiple_of(p * block, block), block)
        slot = jnp.maximum(p - 1, 0)
        return [
            pltpu.make_async_copy(out_seq.at[part], out_ref.at[slot], local.at[0]),
            pltpu.make_async_copy(grad_seq.at[part], gin_ref.at[slot], local.at[1]),
        ]

    def copy_d(c):
        return pltpu.make_async_remote_copy(
            give.at[c % 2], d_recv.at[c], d_ss.at[c], d_rs.at[c], device_id=sib, device_id_type=MESH
        )

    def copy_y(c):
        return pltpu.make_async_remote_copy(
            y_send.at[c], y_recv.at[c], y_ss.at[c], y_rs.at[c], device_id=ypeer, device_id_type=MESH
        )

    def copy_x(c):
        return pltpu.make_async_remote_copy(
            x_send.at[c], x_recv.at[c], x_ss.at[c], x_rs.at[c], device_id=xpeer, device_id_type=MESH
        )

    def part_of(k):
        return pl.ds(pl.multiple_of(k * piece, piece), piece)

    def copy_z(c, j):
        return pltpu.make_async_remote_copy(
            z_send.at[c, part_of((z + j) % ZED)], z_recv.at[c, j - 1], z_ss.at[c, j - 1], z_rs.at[c, j - 1],
            device_id=zpeer(j), device_id_type=MESH,
        )

    def copy_w(c, j):
        return pltpu.make_async_remote_copy(
            w_send.at[c], w_recv.at[c, j - 1], w_ss.at[c, j - 1], w_rs.at[c, j - 1],
            device_id=wpeer(j), device_id_type=MESH,
        )

    def copy_g(c, j):
        place = full.at[c, x, part_of(z)]
        return pltpu.make_async_remote_copy(
            place, place, g_ss.at[c, j - 1], g_rs.at[c, j - 1], device_id=zpeer(j), device_id_type=MESH
        )

    def copy_h(c):
        place = full.at[c, x]
        return pltpu.make_async_remote_copy(
            place, place, h_ss.at[c], h_rs.at[c], device_id=xpeer, device_id_type=MESH
        )

    def copy_s(c):
        u, s = c // subs, c % subs
        half = feat // 2
        return [
            pltpu.make_async_copy(
                full.at[c, h],
                sums_hbm.at[
                    pl.ds(pl.multiple_of(s * rows, rows), rows),
                    pl.ds(pl.multiple_of(u * feat + h * half, half), half),
                ],
                s_sem.at[c, h],
            )
            for h in range(2)
        ]

    def make(c):
        u, s = c // subs, c % subs

        def left_rows(q):
            down = feat * q + quarter * u
            rest = ff + feat * ((u >= 2 * tiles).astype(jnp.int32) + (u > 2 * tiles).astype(jnp.int32)) + quarter * q
            start = jnp.where(u < tiles, down, rest) + s * rows
            return left[pl.ds(pl.multiple_of(start, rows), rows), :]

        order = (2 * (1 - y) + core, 2 * y + core, 2 * (1 - y) + 1 - core, 2 * y + 1 - core)
        lhs = jnp.concatenate([left_rows(q) for q in order], axis=0)
        cols = pl.ds(pl.multiple_of(feat * jnp.maximum(u - tiles + 1, 0), feat), feat)
        total = jnp.dot(lhs, right[:, cols], preferred_element_type=F32)
        slot = c % 2
        own[slot, 0] = total[:rows]
        own[slot, 1] = total[rows : 2 * rows]
        give[slot, 0] = total[2 * rows : 3 * rows].astype(BF16)
        give[slot, 1] = total[3 * rows :].astype(BF16)
        copy_d(c).start()

    def stage_y(c):
        copy_d(c).wait()
        slot = c % 2
        y_send[c] = (own[slot, 0] + d_recv[c, 0].astype(F32)).astype(BF16)
        copy_y(c).start()
        y_keep[c % 4] = own[slot, 1] + d_recv[c, 1].astype(F32)

    def stage_x(c):
        copy_y(c).wait()
        half = feat // 2
        total = y_keep[c % 4] + y_recv[c].astype(F32)

        @pl.when(x == 0)
        def _():
            x_send[c] = total[:, half:].astype(BF16)
            x_keep[c % 4] = total[:, :half]

        @pl.when(x == 1)
        def _():
            x_send[c] = total[:, :half].astype(BF16)
            x_keep[c % 4] = total[:, half:]

        copy_x(c).start()

    def stage_z(c):
        copy_x(c).wait()
        total = x_keep[c % 4] + x_recv[c].astype(F32)
        z_send[c] = total.astype(BF16)
        for j in range(1, ZED):
            copy_z(c, j).start()

    def add_z(c):
        for j in range(1, ZED):
            copy_z(c, j).wait()
        total = z_send[c, part_of(z)].astype(F32)
        for j in range(1, ZED):
            total = total + z_recv[c, j - 1].astype(F32)
        return total

    def stage_w(c):
        w_send[c] = add_z(c).astype(BF16)
        for j in range(1, groups):
            copy_w(c, j).start()

    def add_w(c):
        for j in range(1, groups):
            copy_w(c, j).wait()
        total = w_send[c].astype(F32)
        for j in range(1, groups):
            total = total + w_recv[c, j - 1].astype(F32)
        return total

    def stage_g(c):
        full[c, x, part_of(z)] = (add_z(c) if groups == 1 else add_w(c)).astype(BF16)
        for j in range(1, ZED):
            copy_g(c, j).start()

    def stage_h(c):
        for j in range(1, ZED):
            copy_g(c, j).wait()
        copy_h(c).start()

    def stage_s(c):
        copy_h(c).wait()
        for copy in copy_s(c):
            copy.start()

    ways = [[sib], [ypeer], [xpeer], [zpeer(j) for j in range(1, ZED)]]
    if groups > 1:
        ways.append([wpeer(j) for j in range(1, groups)])
    firsts = [sum(len(way) for way in ways[:i]) for i in range(len(ways))]

    def vector_copies(i):
        return [
            pltpu.make_async_remote_copy(
                vec_ref.at[i], vec_recv.at[firsts[i] + n], v_ss.at[firsts[i] + n], v_rs.at[firsts[i] + n],
                device_id=device, device_id_type=MESH,
            )
            for n, device in enumerate(ways[i])
        ]

    def vector_step(i):
        if i == 0:
            vec_ref[0] = vec_in[...]
        else:
            for copy in vector_copies(i - 1):
                copy.wait()
            total = vec_ref[i - 1]
            for n in range(len(ways[i - 1])):
                total = total + vec_recv[firsts[i - 1] + n]
            vec_ref[i] = total
        if i < len(ways):
            for copy in vector_copies(i):
                copy.start()

    stages = [make, stage_y, stage_x, stage_z] + ([stage_w] if groups > 1 else []) + [stage_g, stage_h, stage_s]
    offsets = [sum(lags[: i + 1]) for i in range(len(stages))]

    def step(t, carry):
        u, s = t // subs, t % subs
        for k in range(len(loads_r)):
            first = 0 if k == 0 else (tiles - 1 + k) * subs

            @pl.when(t == first)
            def _(k=k):
                loads_r[k].wait()

        for k, first in enumerate((0, tiles * subs, 2 * tiles * subs, (2 * tiles + 1) * subs)):
            @pl.when(t == first)
            def _(k=k):
                loads_l[k].wait()

        for stage, offset in zip(stages, offsets):
            c = t - offset

            @pl.when((c >= 0) & (c < chunks))
            def _(stage=stage, c=c):
                stage(c)

        for i in range(len(ways) + 1):
            @pl.when(t == 2 + 3 * i)
            def _(i=i):
                vector_step(i)

        @pl.when(t == 1)
        def _():
            @pl.when(p > 0)
            def _():
                for j in range(1, size):
                    for copy in result_copies(j):
                        copy.start()
                for copy in own_results():
                    copy.start()

        return carry

    lax.fori_loop(0, chunks + offsets[-1], step, 0)

    @pl.when(p > 0)
    def _():
        for copy in own_results():
            copy.wait()
        for j in range(1, size):
            for copy in result_copies(j):
                copy.wait_send()

    for j in range(1, size):
        source = (p + size - j) % size

        @pl.when(source > 0)
        def _(j=j, source=source):
            for n, dst in enumerate((out_ref, gin_ref)):
                pltpu.make_async_copy(dst.at[source - 1], dst.at[source - 1], o_rs.at[n, j - 1]).wait()

    def finish(c, carry):
        for copy in copy_s(c):
            copy.wait()
        return carry

    lax.fori_loop(0, chunks, finish, 0)


def run_reduce(rows, lags, groups, left, right, out_seq, grad_seq, vec, slots):
    seq, feat = out_seq.shape
    ff = left.shape[0] - 3 * feat
    quarter = feat // 4
    units = (2 * ff + 4 * feat) // feat
    chunks = units * (quarter // rows)
    piece = rows // ZED
    half = feat // 2
    steps = 4 + (groups > 1)
    landings = 6 + (groups - 1)
    more = max(groups - 1, 1)
    dma = pltpu.SemaphoreType.DMA
    block = seq // (slots + 1)
    local_block = jax.ShapeDtypeStruct((slots, block, feat), BF16)
    return pl.pallas_call(
        functools.partial(reduce_kernel, (feat, ff, rows, lags, groups)),
        out_shape=(
            jax.ShapeDtypeStruct((quarter, units * feat), BF16),
            local_block,
            local_block,
            jax.ShapeDtypeStruct((steps + 1, 8, feat), F32),
        ),
        in_specs=[ANY, ANY, VMEM, VMEM, VMEM],
        out_specs=(ANY, VMEM, VMEM, VMEM),
        scratch_shapes=[
            pltpu.VMEM(left.shape, BF16),
            pltpu.VMEM(right.shape, BF16),
            pltpu.VMEM((2, 2, rows, feat), F32),
            pltpu.VMEM((2, 2, rows, feat), BF16),
            pltpu.VMEM((chunks, 2, rows, feat), BF16),
            pltpu.VMEM((chunks, rows, feat), BF16),
            pltpu.VMEM((4, rows, feat), F32),
            pltpu.VMEM((chunks, rows, feat), BF16),
            pltpu.VMEM((chunks, rows, half), BF16),
            pltpu.VMEM((4, rows, half), F32),
            pltpu.VMEM((chunks, rows, half), BF16),
            pltpu.VMEM((chunks, rows, half), BF16),
            pltpu.VMEM((chunks, ZED - 1, piece, half), BF16),
            pltpu.VMEM((chunks if groups > 1 else 1, piece, half), BF16),
            pltpu.VMEM((chunks if groups > 1 else 1, more, piece, half), BF16),
            pltpu.VMEM((chunks, 2, rows, half), BF16),
            pltpu.VMEM((landings, 8, feat), F32),
            dma((4,)), dma((units,)),
            dma((chunks,)), dma((chunks,)), dma((chunks,)), dma((chunks,)), dma((chunks,)), dma((chunks,)),
            dma((chunks, ZED - 1)), dma((chunks, ZED - 1)),
            dma((chunks, more)), dma((chunks, more)),
            dma((chunks, ZED - 1)), dma((chunks, ZED - 1)),
            dma((chunks,)), dma((chunks,)), dma((chunks, 2)),
            dma((2, slots)), dma((2, slots)), dma((landings,)), dma((landings,)), dma((2,)),
        ],
        compiler_params=pltpu.CompilerParams(
            collective_id=1, has_side_effects=True, vmem_limit_bytes=58 * 2**20
        ),
    )(left, right, out_seq, grad_seq, vec)


def shards(
    inputs, lengths, w_qkv, w_out, w_up, w_down, norm1_gain, norm1_shift, norm2_gain, norm2_shift, pass_embed, cotangent
):
    p = lax.axis_index("pipe")
    slots, block, feat = inputs.shape
    ff = w_up.shape[1]
    groups = lax.axis_size("dp") // (2 * ZED)
    x, cot = run_exchange(inputs, cotangent)
    length = lax.dynamic_slice_in_dim(lengths, jnp.maximum(p - 1, 0), 1, 0)
    left, right, out_seq, grad_seq, vec = run_chain(
        x, cot, length, norm1_gain, norm1_shift, norm2_gain, norm2_shift, pass_embed, w_qkv, w_out, w_up, w_down
    )
    sums, block_out, input_grads, vecs = run_reduce(
        ROWS, LAGS[: 7 + (groups > 1)], groups, left, right, out_seq, grad_seq, vec, slots
    )
    quarter = feat // 4
    tiles = ff // feat
    down = jnp.concatenate([sums[:, j * feat : (j + 1) * feat] for j in range(tiles)], axis=0).astype(F32)
    up = sums[:, ff : 2 * ff].astype(F32)
    out = sums[:, 2 * ff : 2 * ff + feat].astype(F32)
    qkv = sums[:, 2 * ff + feat :].astype(F32)
    vector = lax.dynamic_slice_in_dim(vecs[-1], p * quarter, quarter, 1)
    return (block_out, input_grads, qkv, out, up, down) + tuple(vector[i] for i in range(5))


ROWS = 64
LAGS = (0, 1, 3, 2, 3, 3, 2, 2)


def solution(mesh):
    rep = P()
    seqs = P("dp", "pipe", None)
    return jax.shard_map(
        shards,
        mesh=mesh,
        in_specs=(seqs, P("dp")) + (rep,) * 9 + (seqs,),
        out_specs=(seqs, seqs) + (P("pipe", None),) * 4 + (P("pipe"),) * 5,
        check_vma=False,
    )
```

```python
import functools

import jax
import jax.numpy as jnp
from jax import lax
from jax.experimental import pallas as pl
from jax.experimental.pallas import tpu as pltpu
from jax.sharding import PartitionSpec as P

MESH = pl.DeviceIdType.MESH
HEADS = 12
HEAD = 64
F32 = jnp.float32
BF16 = jnp.bfloat16
ANY = pl.BlockSpec(memory_space=pl.ANY)
VMEM = pl.BlockSpec(memory_space=pltpu.VMEM)
SMEM = pl.BlockSpec(memory_space=pltpu.SMEM)


def dot(left, right):
    return jnp.dot(left, right, preferred_element_type=F32)


def dot_nt(left, right):
    return lax.dot_general(left, right, (((1,), (1,)), ((), ())), preferred_element_type=F32)


def normalize(values):
    center = values - jnp.mean(values, axis=-1, keepdims=True)
    scale = lax.rsqrt(jnp.mean(center * center, axis=-1, keepdims=True) + 1e-05)
    return center * scale, scale


ZED = 4
SLOTS = 8
ROWS = 64
LAGS = (0, 1, 3, 2, 3, 3, 2, 2)
EARLY = (2, 4)


def block_kernel(
    dims, in_hbm, cot_hbm, len_ref, gain1_ref, shift1_ref, gain2_ref, shift2_ref, embed_ref,
    wqkv_hbm, wout_hbm, wup_hbm, wdown_hbm,
    sums_hbm, out_ref, gin_ref, vec_ref,
    x_ref, cot_ref, out_seq, grad_seq, vec_part, vec_sum,
    wqkv, wout, wup, wdown, left, right, qkv, vt, kt, lse, gp, mixed, state, ctx,
    dk_more, dv_more, dqt, dctx, bias,
    own, give, d_recv, y_send, y_keep, y_recv, x_send, x_keep, x_recv,
    z_send, z_recv, w_send, w_recv, full, vec_recv,
    w_sem, i_ss, i_rs, d_ss, d_rs, y_ss, y_rs, x_ss, x_rs, z_ss, z_rs, w_ss, w_rs, g_ss, g_rs, h_ss, h_rs, s_sem,
    o_ss, o_rs, v_ss, v_rs, local,
):
    rows, lags, groups = dims
    slots, block, feat = in_hbm.shape
    size = slots + 1
    seq = size * block
    ff = wup.shape[1]
    tiles = ff // feat
    half = feat // 6
    units = (2 * ff + 4 * feat) // feat
    quarter = feat // 4
    subs = quarter // rows
    chunks = units * subs
    piece = rows // ZED
    g = lax.axis_index("dp")
    p = lax.axis_index("pipe")
    core, y = p % 2, p // 2
    x, z, w = g % 2, (g // 2) % ZED, g // (2 * ZED)
    sib = (g, p + 1 - 2 * core)
    ypeer = (g, p + 2 - 4 * y)
    diag = (g, 3 - p)
    xpeer = (g + 1 - 2 * x, p)

    def zpeer(j):
        return (g + 2 * ((z + j) % ZED - z), p)

    def wpeer(j):
        return (g + 2 * ZED * ((w + j) % groups - w), p)

    everyone = [sib, ypeer, diag, xpeer] + [zpeer(j) for j in range(1, ZED)] + [wpeer(j) for j in range(1, groups)]

    weight_copies = [
        pltpu.make_async_copy(src, dst, w_sem.at[i])
        for i, (src, dst) in enumerate(
            ((wqkv_hbm, wqkv), (wout_hbm, wout), (wup_hbm, wup), (wdown_hbm, wdown))
        )
    ]
    for copy in weight_copies:
        copy.start()

    barrier = pltpu.get_barrier_semaphore()
    for device in everyone:
        pl.semaphore_signal(barrier, inc=1, device_id=device, device_id_type=MESH)
    pl.semaphore_wait(barrier, len(everyone))

    mine = pl.ds(pl.multiple_of(p * block, block), block)

    def input_copies(j):
        peer = (p + j) % size
        slot = jnp.maximum(peer - 1, 0)
        return [
            pltpu.make_async_remote_copy(
                src.at[slot], dst.at[mine], i_ss.at[n, j - 1], i_rs.at[n, j - 1],
                device_id=(g, peer), device_id_type=MESH,
            )
            for n, (src, dst) in enumerate(((in_hbm, x_ref), (cot_hbm, cot_ref)))
        ]

    def own_inputs():
        slot = jnp.maximum(p - 1, 0)
        return [
            pltpu.make_async_copy(src.at[slot], dst.at[mine], local.at[n])
            for n, (src, dst) in enumerate(((in_hbm, x_ref), (cot_hbm, cot_ref)))
        ]

    def wait_inputs(n):
        @pl.when(p > 0)
        def _():
            own_inputs()[n].wait()
            for j in range(1, size):
                input_copies(j)[n].wait_recv()

        for j in range(1, size):
            @pl.when((p + j) % size > 0)
            def _(j=j):
                input_copies(j)[n].wait_send()

    for n in range(2):
        for j in range(1, size):
            @pl.when((p + j) % size > 0)
            def _(j=j, n=n):
                input_copies(j)[n].start()

    @pl.when(p > 0)
    def _():
        for copy in own_inputs():
            copy.start()

    @pl.when(p == 0)
    def _():
        x_ref[...] = jnp.zeros(x_ref.shape, x_ref.dtype)
        cot_ref[...] = jnp.zeros(cot_ref.shape, cot_ref.dtype)

    slots, block, _ = out_ref.shape
    size = slots + 1

    def result_copies(j):
        peer = (p + j) % size
        slot = jnp.maximum(p - 1, 0)
        part = pl.ds(pl.multiple_of(peer * block, block), block)
        return [
            pltpu.make_async_remote_copy(
                src.at[part], dst.at[slot], o_ss.at[n, j - 1], o_rs.at[n, j - 1],
                device_id=(g, peer), device_id_type=MESH,
            )
            for n, (src, dst) in enumerate(((out_seq, out_ref), (grad_seq, gin_ref)))
        ]

    def own_results():
        part = pl.ds(pl.multiple_of(p * block, block), block)
        slot = jnp.maximum(p - 1, 0)
        return [
            pltpu.make_async_copy(out_seq.at[part], out_ref.at[slot], local.at[0]),
            pltpu.make_async_copy(grad_seq.at[part], gin_ref.at[slot], local.at[1]),
        ]

    def copy_d(c):
        return pltpu.make_async_remote_copy(
            give.at[c % 2], d_recv.at[c % SLOTS], d_ss.at[c % SLOTS], d_rs.at[c % SLOTS], device_id=sib, device_id_type=MESH
        )

    def copy_y(c):
        return pltpu.make_async_remote_copy(
            y_send.at[c % SLOTS], y_recv.at[c % SLOTS], y_ss.at[c % SLOTS], y_rs.at[c % SLOTS], device_id=ypeer, device_id_type=MESH
        )

    def copy_x(c):
        return pltpu.make_async_remote_copy(
            x_send.at[c % SLOTS], x_recv.at[c % SLOTS], x_ss.at[c % SLOTS], x_rs.at[c % SLOTS], device_id=xpeer, device_id_type=MESH
        )

    def part_of(k):
        return pl.ds(pl.multiple_of(k * piece, piece), piece)

    def copy_z(c, j):
        return pltpu.make_async_remote_copy(
            z_send.at[c % SLOTS, part_of((z + j) % ZED)], z_recv.at[c % SLOTS, j - 1], z_ss.at[c % SLOTS, j - 1], z_rs.at[c % SLOTS, j - 1],
            device_id=zpeer(j), device_id_type=MESH,
        )

    def copy_w(c, j):
        return pltpu.make_async_remote_copy(
            w_send.at[c % SLOTS], w_recv.at[c % SLOTS, j - 1], w_ss.at[c % SLOTS, j - 1], w_rs.at[c % SLOTS, j - 1],
            device_id=wpeer(j), device_id_type=MESH,
        )

    def copy_g(c, j):
        place = full.at[c, x, part_of(z)]
        return pltpu.make_async_remote_copy(
            place, place, g_ss.at[c, j - 1], g_rs.at[c, j - 1], device_id=zpeer(j), device_id_type=MESH
        )

    def copy_h(c):
        place = full.at[c, x]
        return pltpu.make_async_remote_copy(
            place, place, h_ss.at[c], h_rs.at[c], device_id=xpeer, device_id_type=MESH
        )

    def copy_s(c):
        u, s = c // subs, c % subs
        half = feat // 2
        return [
            pltpu.make_async_copy(
                full.at[c, h],
                sums_hbm.at[
                    pl.ds(pl.multiple_of(s * rows, rows), rows),
                    pl.ds(pl.multiple_of(u * feat + h * half, half), half),
                ],
                s_sem.at[c, h],
            )
            for h in range(2)
        ]

    def make(c):
        u, s = c // subs, c % subs

        def left_rows(q):
            down = feat * q + quarter * u
            rest = ff + feat * ((u >= 2 * tiles).astype(jnp.int32) + (u > 2 * tiles).astype(jnp.int32)) + quarter * q
            start = jnp.where(u < tiles, down, rest) + s * rows
            return left[pl.ds(pl.multiple_of(start, rows), rows), :]

        order = (2 * (1 - y) + core, 2 * y + core, 2 * (1 - y) + 1 - core, 2 * y + 1 - core)
        lhs = jnp.concatenate([left_rows(q) for q in order], axis=0)
        cols = pl.ds(pl.multiple_of(feat * jnp.maximum(u - tiles + 1, 0), feat), feat)
        total = jnp.dot(lhs, right[:, cols], preferred_element_type=F32)
        slot = c % 2
        own[slot, 0] = total[:rows]
        own[slot, 1] = total[rows : 2 * rows]
        give[slot, 0] = total[2 * rows : 3 * rows].astype(BF16)
        give[slot, 1] = total[3 * rows :].astype(BF16)
        copy_d(c).start()

    def stage_y(c):
        copy_d(c).wait()
        slot = c % 2
        y_send[c % SLOTS] = (own[slot, 0] + d_recv[c % SLOTS, 0].astype(F32)).astype(BF16)
        copy_y(c).start()
        y_keep[c % SLOTS] = own[slot, 1] + d_recv[c % SLOTS, 1].astype(F32)

    def stage_x(c):
        copy_y(c).wait()
        half = feat // 2
        total = y_keep[c % SLOTS] + y_recv[c % SLOTS].astype(F32)

        @pl.when(x == 0)
        def _():
            x_send[c % SLOTS] = total[:, half:].astype(BF16)
            x_keep[c % SLOTS] = total[:, :half]

        @pl.when(x == 1)
        def _():
            x_send[c % SLOTS] = total[:, :half].astype(BF16)
            x_keep[c % SLOTS] = total[:, half:]

        copy_x(c).start()

    def stage_z(c):
        copy_x(c).wait()
        total = x_keep[c % SLOTS] + x_recv[c % SLOTS].astype(F32)
        z_send[c % SLOTS] = total.astype(BF16)
        for j in range(1, ZED):
            copy_z(c, j).start()

    def add_z(c):
        for j in range(1, ZED):
            copy_z(c, j).wait()
        total = z_send[c % SLOTS, part_of(z)].astype(F32)
        for j in range(1, ZED):
            total = total + z_recv[c % SLOTS, j - 1].astype(F32)
        return total

    def stage_w(c):
        w_send[c % SLOTS] = add_z(c).astype(BF16)
        for j in range(1, groups):
            copy_w(c, j).start()

    def add_w(c):
        for j in range(1, groups):
            copy_w(c, j).wait()
        total = w_send[c % SLOTS].astype(F32)
        for j in range(1, groups):
            total = total + w_recv[c % SLOTS, j - 1].astype(F32)
        return total

    def stage_g(c):
        full[c, x, part_of(z)] = (add_z(c) if groups == 1 else add_w(c)).astype(BF16)
        for j in range(1, ZED):
            copy_g(c, j).start()

    def stage_h(c):
        for j in range(1, ZED):
            copy_g(c, j).wait()
        copy_h(c).start()

    def stage_s(c):
        copy_h(c).wait()
        for copy in copy_s(c):
            copy.start()

    ways = [[sib], [ypeer], [xpeer], [zpeer(j) for j in range(1, ZED)]]
    if groups > 1:
        ways.append([wpeer(j) for j in range(1, groups)])
    firsts = [sum(len(way) for way in ways[:i]) for i in range(len(ways))]

    def vector_copies(i):
        return [
            pltpu.make_async_remote_copy(
                vec_sum.at[i], vec_recv.at[firsts[i] + n], v_ss.at[firsts[i] + n], v_rs.at[firsts[i] + n],
                device_id=device, device_id_type=MESH,
            )
            for n, device in enumerate(ways[i])
        ]

    def vector_step(i):
        if i == 0:
            vec_sum[0] = vec_part[...]
        else:
            for copy in vector_copies(i - 1):
                copy.wait()
            total = vec_sum[i - 1]
            for n in range(len(ways[i - 1])):
                total = total + vec_recv[firsts[i - 1] + n]
            vec_sum[i] = total
        if i < len(ways):
            for copy in vector_copies(i):
                copy.start()

    stages = [make, stage_y, stage_x, stage_z] + ([stage_w] if groups > 1 else []) + [stage_g, stage_h, stage_s]
    offsets = [sum(lags[: i + 1]) for i in range(len(stages))]

    def step(t, carry):
        for stage, offset in zip(stages, offsets):
            c = t - offset

            @pl.when((c >= 0) & (c < chunks))
            def _(stage=stage, c=c):
                stage(c)

        return carry

    def run_steps(first, end):
        lax.fori_loop(first, end, step, 0)

    length = len_ref[jnp.maximum(p - 1, 0)]
    keys = lax.broadcasted_iota(jnp.int32, (seq, seq), 0)
    queries = lax.broadcasted_iota(jnp.int32, (seq, seq), 1)
    bias[...] = jnp.where((keys <= queries) & (keys < length), 0.0, -1e30).astype(F32)
    inside = (lax.broadcasted_iota(jnp.int32, (seq, 1), 0) < length).astype(F32)
    low_lanes = lax.broadcasted_iota(jnp.int32, (seq, half), 1) < HEAD

    def pick(values, head):
        zero = jnp.zeros_like(values)
        return jnp.where(low_lanes, values, zero) if head == 0 else jnp.where(low_lanes, zero, values)

    def rows_of(i):
        return pl.ds(i * seq, seq)

    def put_left(offset, i, values):
        left[pl.ds(offset, values.shape[1]), rows_of(i)] = values.T

    N2, CTX, N1 = ff, ff + feat, ff + 2 * feat
    HID, ATT, QKV = feat, feat + ff, 2 * feat + ff

    def forward(i):
        value = state[i]
        n1 = (normalize(value)[0] * gain1_ref[...] + shift1_ref[...]).astype(BF16)
        put_left(N1, i, n1)
        if i == 0:
            weight_copies[0].wait()
        for j in range(3):
            part = dot(n1, wqkv[:, j * feat : (j + 1) * feat])
            if j == 0:
                part = part * HEAD ** (-0.5)
            part = part.astype(BF16)
            qkv[i, :, j * feat : (j + 1) * feat] = part
            if j == 1:
                kt[i] = part.T
            if j == 2:
                vt[i] = part.T

        def pair(hp, carry):
            lanes = pl.ds(pl.multiple_of(hp * half, half), half)
            q2 = qkv[i, :, lanes]
            for head in range(2):
                qm = pick(q2, head)
                scores = []
                for b in range(i + 1):
                    k2 = qkv[b, :, pl.ds(pl.multiple_of(feat + hp * half, half), half)]
                    scores.append(dot_nt(k2, qm) + bias[...])
                top = jnp.max(scores[0], axis=0, keepdims=True)
                for s in scores[1:]:
                    top = jnp.maximum(top, jnp.max(s, axis=0, keepdims=True))
                weights = [jnp.exp(s - top) for s in scores]
                total = jnp.sum(weights[0], axis=0, keepdims=True)
                for w in weights[1:]:
                    total = total + jnp.sum(w, axis=0, keepdims=True)
                inv = 1.0 / total
                lse[i, pl.ds(2 * hp + head, 1), :] = top + jnp.log(total)
                rows = pl.ds(pl.multiple_of(hp * half + head * HEAD, HEAD), HEAD)
                acc = None
                for b in range(i + 1):
                    term = dot(vt[b, rows, :], (weights[b] * inv).astype(BF16))
                    acc = term if acc is None else acc + term
                left[pl.ds(pl.multiple_of(CTX + hp * half + head * HEAD, HEAD), HEAD), rows_of(i)] = acc.astype(BF16)
            return carry

        lax.fori_loop(0, feat // half, pair, 0)
        ctx[...] = left[pl.ds(CTX, feat), rows_of(i)].T
        if i == 0:
            weight_copies[1].wait()
        mix = state[i] + dot(ctx[...], wout[...])
        mixed[i] = mix
        n2 = (normalize(mix)[0] * gain2_ref[...] + shift2_ref[...]).astype(BF16)
        put_left(N2, i, n2)
        if i == 0:
            weight_copies[2].wait()
            weight_copies[3].wait()
        acc = mix
        for j in range(tiles):
            u = dot(n2, wup[:, j * feat : (j + 1) * feat])
            c = 0.7978845608028654
            square = u * u
            th = jnp.tanh(c * u * (1.0 + 0.044715 * square))
            halfp = 0.5 + 0.5 * th
            active = (u * halfp).astype(BF16)
            slope = halfp + 0.5 * u * (1.0 - th * th) * (c * (1.0 + 3 * 0.044715 * square))
            gp[i, :, j * feat : (j + 1) * feat] = slope.astype(BF16)
            put_left(j * feat, i, active)
            acc = acc + dot(active, wdown[j * feat : (j + 1) * feat, :])
        return acc

    def norm_back(values, d_out, gain, slot, first):
        norm, scale = normalize(values)
        g_gain = jnp.sum(d_out * norm, axis=0, keepdims=True)
        g_shift = jnp.sum(d_out, axis=0, keepdims=True)
        if first:
            vec_part[slot : slot + 1, :] = g_gain
            vec_part[slot + 1 : slot + 2, :] = g_shift
        else:
            vec_part[slot : slot + 1, :] += g_gain
            vec_part[slot + 1 : slot + 2, :] += g_shift
        t = d_out * gain
        return scale * (t - jnp.mean(t, axis=-1, keepdims=True) - norm * jnp.mean(t * norm, axis=-1, keepdims=True))

    def backward(i, grad):
        branch = grad.astype(BF16)
        right[rows_of(i), 0:feat] = branch
        if i == 0:
            run_steps(0, EARLY[0])
        acc = None
        for j in range(tiles):
            d_active = dot_nt(branch, wdown[j * feat : (j + 1) * feat, :])
            d_hidden = (d_active * gp[i, :, j * feat : (j + 1) * feat].astype(F32)).astype(BF16)
            right[rows_of(i), HID + j * feat : HID + (j + 1) * feat] = d_hidden
            term = dot_nt(d_hidden, wup[:, j * feat : (j + 1) * feat])
            acc = term if acc is None else acc + term
        if i == 0:
            run_steps(EARLY[0], EARLY[1])
        d_mixed = grad + norm_back(mixed[i], acc, gain2_ref[...], 2, i == 1)
        d_attn = d_mixed.astype(BF16)
        right[rows_of(i), ATT : ATT + feat] = d_attn
        dctx[...] = dot_nt(d_attn, wout[...]).astype(BF16)

        def pair(hp, carry):
            lanes = pl.ds(pl.multiple_of(hp * half, half), half)
            q2 = qkv[i, :, lanes]
            do2 = dctx[:, lanes]
            dk = [None] * (i + 1)
            dv = [None] * (i + 1)
            for head in range(2):
                qm = pick(q2, head)
                dom = pick(do2, head)
                row = lse[i, pl.ds(2 * hp + head, 1), :]
                soft, d_soft = [], []
                inner = None
                for b in range(i + 1):
                    k2 = qkv[b, :, pl.ds(pl.multiple_of(feat + hp * half, half), half)]
                    v2 = qkv[b, :, pl.ds(pl.multiple_of(2 * feat + hp * half, half), half)]
                    soft.append(jnp.exp(dot_nt(k2, qm) + (bias[...] - row)))
                    d_soft.append(dot_nt(v2, dom))
                    term = jnp.sum(soft[b] * d_soft[b], axis=0, keepdims=True)
                    inner = term if inner is None else inner + term
                rows = pl.ds(pl.multiple_of(hp * half + head * HEAD, HEAD), HEAD)
                dq = None
                for b in range(i + 1):
                    d_score = (soft[b] * (d_soft[b] - inner)).astype(BF16)
                    term_v = dot(soft[b].astype(BF16), dom)
                    term_k = dot(d_score, qm)
                    term_q = dot(kt[b, rows, :], d_score)
                    dv[b] = term_v if dv[b] is None else dv[b] + term_v
                    dk[b] = term_k if dk[b] is None else dk[b] + term_k
                    dq = term_q if dq is None else dq + term_q
                dqt[rows, :] = (dq * HEAD ** (-0.5)).astype(BF16)
            dk_own, dv_own = dk[i], dv[i]
            if i == 1:
                dk_more[:, lanes] = dk[0]
                dv_more[:, lanes] = dv[0]
            else:
                dk_own = dk_own + dk_more[:, lanes]
                dv_own = dv_own + dv_more[:, lanes]
            right[rows_of(i), pl.ds(pl.multiple_of(QKV + feat + hp * half, half), half)] = dk_own.astype(BF16)
            right[rows_of(i), pl.ds(pl.multiple_of(QKV + 2 * feat + hp * half, half), half)] = dv_own.astype(BF16)
            if i == 0:
                @pl.when(hp % 2 == 1)
                def _():
                    step(EARLY[1] + hp // 2, 0)
            return carry

        lax.fori_loop(0, feat // half, pair, 0)
        right[rows_of(i), QKV : QKV + feat] = dqt[...].T
        d_normed = None
        for j in range(3):
            term = dot_nt(
                right[rows_of(i), QKV + j * feat : QKV + (j + 1) * feat], wqkv[:, j * feat : (j + 1) * feat]
            )
            d_normed = term if d_normed is None else d_normed + term
        return d_mixed + norm_back(state[i], d_normed, gain1_ref[...], 0, i == 1)

    wait_inputs(0)
    state[0] = x_ref[...].astype(F32)
    first = forward(0)
    state[1] = first.astype(BF16).astype(F32) + embed_ref[...]
    second = forward(1)
    out_seq[...] = (second * inside).astype(BF16)
    wait_inputs(1)

    def send_results(n):
        @pl.when(p > 0)
        def _():
            for j in range(1, size):
                result_copies(j)[n].start()
            own_results()[n].start()

    send_results(0)
    d_carry = backward(1, cot_ref[...].astype(F32) * inside)
    vec_part[4:5, :] = jnp.sum(d_carry, axis=0, keepdims=True)
    vec_part[5:8, :] = jnp.zeros((3, feat), F32)
    d_state = backward(0, d_carry.astype(BF16).astype(F32))
    grad_seq[...] = d_state.astype(BF16)
    send_results(1)

    begun = EARLY[1] + 3
    vector_step(0)

    def late_step(t, carry):
        step(t, 0)
        for i in range(1, len(ways) + 1):
            @pl.when(t == begun + 3 * i)
            def _(i=i):
                vector_step(i)

        return carry

    lax.fori_loop(begun, chunks + offsets[-1], late_step, 0)
    vec_ref[...] = vec_sum[len(ways)]

    @pl.when(p > 0)
    def _():
        for copy in own_results():
            copy.wait()
        for j in range(1, size):
            for copy in result_copies(j):
                copy.wait_send()

    for j in range(1, size):
        source = (p + size - j) % size

        @pl.when(source > 0)
        def _(j=j, source=source):
            for n, dst in enumerate((out_ref, gin_ref)):
                pltpu.make_async_copy(dst.at[source - 1], dst.at[source - 1], o_rs.at[n, j - 1]).wait()

    def finish(c, carry):
        for copy in copy_s(c):
            copy.wait()
        return carry

    lax.fori_loop(0, chunks, finish, 0)


def run_block(inputs, cotangent, lengths, vectors, w_qkv, w_out, w_up, w_down, rows, lags, groups):
    slots, block, feat = inputs.shape
    ff = w_up.shape[1]
    seq = (slots + 1) * block
    quarter = feat // 4
    units = (2 * ff + 4 * feat) // feat
    chunks = units * (quarter // rows)
    piece = rows // ZED
    half = feat // 2
    ways = 4 + (groups > 1)
    landings = 6 + (groups - 1)
    more = max(groups - 1, 1)
    dma = pltpu.SemaphoreType.DMA
    local_block = jax.ShapeDtypeStruct((slots, block, feat), BF16)
    left_rows = ff + 3 * feat
    right_cols = 5 * feat + ff
    return pl.pallas_call(
        functools.partial(block_kernel, (rows, lags, groups)),
        out_shape=(
            jax.ShapeDtypeStruct((quarter, units * feat), BF16),
            local_block,
            local_block,
            jax.ShapeDtypeStruct((8, feat), F32),
        ),
        in_specs=[ANY, ANY, SMEM] + [VMEM] * 5 + [ANY] * 4,
        out_specs=(ANY, VMEM, VMEM, VMEM),
        scratch_shapes=[
            pltpu.VMEM((seq, feat), BF16),
            pltpu.VMEM((seq, feat), BF16),
            pltpu.VMEM((seq, feat), BF16),
            pltpu.VMEM((seq, feat), BF16),
            pltpu.VMEM((8, feat), F32),
            pltpu.VMEM((ways + 1, 8, feat), F32),
            pltpu.VMEM(w_qkv.shape, BF16),
            pltpu.VMEM(w_out.shape, BF16),
            pltpu.VMEM(w_up.shape, BF16),
            pltpu.VMEM(w_down.shape, BF16),
            pltpu.VMEM((left_rows, 2 * seq), BF16),
            pltpu.VMEM((2 * seq, right_cols), BF16),
            pltpu.VMEM((2, seq, 3 * feat), BF16),
            pltpu.VMEM((2, feat, seq), BF16),
            pltpu.VMEM((2, feat, seq), BF16),
            pltpu.VMEM((2, 16, seq), F32),
            pltpu.VMEM((2, seq, ff), BF16),
            pltpu.VMEM((2, seq, feat), F32),
            pltpu.VMEM((2, seq, feat), F32),
            pltpu.VMEM((seq, feat), BF16),
            pltpu.VMEM((seq, feat), F32),
            pltpu.VMEM((seq, feat), F32),
            pltpu.VMEM((feat, seq), BF16),
            pltpu.VMEM((seq, feat), BF16),
            pltpu.VMEM((seq, seq), F32),
            pltpu.VMEM((2, 2, rows, feat), F32),
            pltpu.VMEM((2, 2, rows, feat), BF16),
            pltpu.VMEM((SLOTS, 2, rows, feat), BF16),
            pltpu.VMEM((SLOTS, rows, feat), BF16),
            pltpu.VMEM((SLOTS, rows, feat), F32),
            pltpu.VMEM((SLOTS, rows, feat), BF16),
            pltpu.VMEM((SLOTS, rows, half), BF16),
            pltpu.VMEM((SLOTS, rows, half), F32),
            pltpu.VMEM((SLOTS, rows, half), BF16),
            pltpu.VMEM((SLOTS, rows, half), BF16),
            pltpu.VMEM((SLOTS, ZED - 1, piece, half), BF16),
            pltpu.VMEM((SLOTS if groups > 1 else 1, piece, half), BF16),
            pltpu.VMEM((SLOTS if groups > 1 else 1, more, piece, half), BF16),
            pltpu.VMEM((chunks, 2, rows, half), BF16),
            pltpu.VMEM((landings, 8, feat), F32),
            dma((4,)), dma((2, slots)), dma((2, slots)),
            dma((SLOTS,)), dma((SLOTS,)), dma((SLOTS,)), dma((SLOTS,)), dma((SLOTS,)), dma((SLOTS,)),
            dma((SLOTS, ZED - 1)), dma((SLOTS, ZED - 1)),
            dma((SLOTS, more)), dma((SLOTS, more)),
            dma((chunks, ZED - 1)), dma((chunks, ZED - 1)),
            dma((chunks,)), dma((chunks,)), dma((chunks, 2)),
            dma((2, slots)), dma((2, slots)), dma((landings,)), dma((landings,)), dma((2,)),
        ],
        compiler_params=pltpu.CompilerParams(
            collective_id=0, has_side_effects=True, vmem_limit_bytes=60 * 2**20
        ),
    )(inputs, cotangent, lengths, *vectors, w_qkv, w_out, w_up, w_down)


def shards(
    inputs, lengths, w_qkv, w_out, w_up, w_down, norm1_gain, norm1_shift, norm2_gain, norm2_shift, pass_embed, cotangent
):
    p = lax.axis_index("pipe")
    slots, block, feat = inputs.shape
    ff = w_up.shape[1]
    groups = lax.axis_size("dp") // (2 * ZED)
    vectors = [v.reshape(1, feat) for v in (norm1_gain, norm1_shift, norm2_gain, norm2_shift, pass_embed)]
    sums, block_out, input_grads, vec = run_block(
        inputs, cotangent, lengths, vectors, w_qkv, w_out, w_up, w_down, ROWS, LAGS[: 7 + (groups > 1)], groups
    )
    quarter = feat // 4
    tiles = ff // feat
    down = jnp.concatenate([sums[:, j * feat : (j + 1) * feat] for j in range(tiles)], axis=0).astype(F32)
    up = sums[:, ff : 2 * ff].astype(F32)
    out = sums[:, 2 * ff : 2 * ff + feat].astype(F32)
    qkv = sums[:, 2 * ff + feat :].astype(F32)
    vector = lax.dynamic_slice_in_dim(vec, p * quarter, quarter, 1)
    return (block_out, input_grads, qkv, out, up, down) + tuple(vector[i] for i in range(5))


def solution(mesh):
    rep = P()
    seqs = P("dp", "pipe", None)
    return jax.shard_map(
        shards,
        mesh=mesh,
        in_specs=(seqs, P("dp")) + (rep,) * 9 + (seqs,),
        out_specs=(seqs, seqs) + (P("pipe", None),) * 4 + (P("pipe"),) * 5,
        check_vma=False,
    )
```

```python
import functools

import jax
import jax.numpy as jnp
from jax import lax
from jax.experimental import pallas as pl
from jax.experimental.pallas import tpu as pltpu
from jax.sharding import PartitionSpec as P

MESH = pl.DeviceIdType.MESH
HEADS = 12
HEAD = 64
F32 = jnp.float32
BF16 = jnp.bfloat16
ANY = pl.BlockSpec(memory_space=pl.ANY)
VMEM = pl.BlockSpec(memory_space=pltpu.VMEM)
SMEM = pl.BlockSpec(memory_space=pltpu.SMEM)


def dot(left, right):
    return jnp.dot(left, right, preferred_element_type=F32)


def dot_nt(left, right):
    return lax.dot_general(left, right, (((1,), (1,)), ((), ())), preferred_element_type=F32)


def row(ref):
    return ref[...].reshape(1, ref.shape[0])


def normalize(values):
    center = values - jnp.mean(values, axis=-1, keepdims=True)
    scale = lax.rsqrt(jnp.mean(center * center, axis=-1, keepdims=True) + 1e-05)
    return center * scale, scale


ZED = 4
SLOTS = 8
STORES = 4
ROWS = 64
LAGS = (0, 1, 3, 2, 3, 3, 2, 2)
EARLY = (2, 4)
FORWARD_PAIRS = 3
BACKWARD_PAIRS = 2


def block_kernel(
    dims, in_ref, given_ref, len_ref, gain1_ref, shift1_ref, gain2_ref, shift2_ref, embed_ref,
    wqkv_hbm, wout_hbm, wup_hbm, wdown_hbm,
    sums_hbm, out_ref, gin_ref, vec_ref,
    x_ref, cot_ref, out_seq, grad_seq, vec_part, vec_sum,
    wqkv, wout, wup, wdown, left, right, qkv, vt, kt, lse, gp, mixed, state, ctx,
    dk_more, dv_more, dqt, dctx, bias,
    own, give, d_recv, y_send, y_keep, y_recv, x_send, x_keep, x_recv,
    z_send, z_recv, w_send, w_recv, full, vec_recv,
    w_sem, i_ss, i_rs, d_ss, d_rs, y_ss, y_rs, x_ss, x_rs, z_ss, z_rs, w_ss, w_rs, g_ss, g_rs, h_ss, h_rs, s_sem,
    o_ss, o_rs, v_ss, v_rs, local,
):
    rows, lags, groups = dims
    slots, block, feat = in_ref.shape
    size = slots + 1
    seq = size * block
    ff = wup.shape[1]
    tiles = ff // feat
    half = feat // 6
    units = (2 * ff + 4 * feat) // feat
    quarter = feat // 4
    subs = quarter // rows
    chunks = units * subs
    piece = rows // ZED
    g = lax.axis_index("dp")
    p = lax.axis_index("pipe")
    core, y = p % 2, p // 2
    x, z, w = g % 2, (g // 2) % ZED, g // (2 * ZED)
    sib = (g, p + 1 - 2 * core)
    ypeer = (g, p + 2 - 4 * y)
    diag = (g, 3 - p)
    xpeer = (g + 1 - 2 * x, p)

    def zpeer(j):
        return (g + 2 * ((z + j) % ZED - z), p)

    def wpeer(j):
        return (g + 2 * ZED * ((w + j) % groups - w), p)

    everyone = [sib, ypeer, diag, xpeer] + [zpeer(j) for j in range(1, ZED)] + [wpeer(j) for j in range(1, groups)]

    weight_copies = [
        pltpu.make_async_copy(src, dst, w_sem.at[i])
        for i, (src, dst) in enumerate(
            ((wqkv_hbm, wqkv), (wout_hbm, wout), (wup_hbm, wup), (wdown_hbm, wdown))
        )
    ]
    for copy in weight_copies:
        copy.start()

    barrier = pltpu.get_barrier_semaphore()
    for device in everyone:
        pl.semaphore_signal(barrier, inc=1, device_id=device, device_id_type=MESH)
    pl.semaphore_wait(barrier, len(everyone))

    mine = pl.ds(pl.multiple_of(p * block, block), block)

    def input_copies(j):
        peer = (p + j) % size
        slot = jnp.maximum(peer - 1, 0)
        return [
            pltpu.make_async_remote_copy(
                src.at[slot], dst.at[mine], i_ss.at[n, j - 1], i_rs.at[n, j - 1],
                device_id=(g, peer), device_id_type=MESH,
            )
            for n, (src, dst) in enumerate(((in_ref, x_ref), (given_ref, cot_ref)))
        ]

    def own_inputs():
        slot = jnp.maximum(p - 1, 0)
        return [
            pltpu.make_async_copy(src.at[slot], dst.at[mine], local.at[n])
            for n, (src, dst) in enumerate(((in_ref, x_ref), (given_ref, cot_ref)))
        ]

    def wait_inputs(n):
        @pl.when(p > 0)
        def _():
            own_inputs()[n].wait()
            for j in range(1, size):
                input_copies(j)[n].wait_recv()

        for j in range(1, size):
            @pl.when((p + j) % size > 0)
            def _(j=j):
                input_copies(j)[n].wait_send()

    for n in range(2):
        for j in range(1, size):
            @pl.when((p + j) % size > 0)
            def _(j=j, n=n):
                input_copies(j)[n].start()

    @pl.when(p > 0)
    def _():
        for copy in own_inputs():
            copy.start()

    @pl.when(p == 0)
    def _():
        x_ref[...] = jnp.zeros(x_ref.shape, x_ref.dtype)
        cot_ref[...] = jnp.zeros(cot_ref.shape, cot_ref.dtype)

    slots, block, _ = out_ref.shape
    size = slots + 1

    def result_copies(j):
        peer = (p + j) % size
        slot = jnp.maximum(p - 1, 0)
        part = pl.ds(pl.multiple_of(peer * block, block), block)
        return [
            pltpu.make_async_remote_copy(
                src.at[part], dst.at[slot], o_ss.at[n, j - 1], o_rs.at[n, j - 1],
                device_id=(g, peer), device_id_type=MESH,
            )
            for n, (src, dst) in enumerate(((out_seq, out_ref), (grad_seq, gin_ref)))
        ]

    def own_results():
        part = pl.ds(pl.multiple_of(p * block, block), block)
        slot = jnp.maximum(p - 1, 0)
        return [
            pltpu.make_async_copy(out_seq.at[part], out_ref.at[slot], local.at[0]),
            pltpu.make_async_copy(grad_seq.at[part], gin_ref.at[slot], local.at[1]),
        ]

    def copy_d(c):
        return pltpu.make_async_remote_copy(
            give.at[c % 2], d_recv.at[c % SLOTS], d_ss.at[c % SLOTS], d_rs.at[c % SLOTS], device_id=sib, device_id_type=MESH
        )

    def copy_y(c):
        return pltpu.make_async_remote_copy(
            y_send.at[c % SLOTS], y_recv.at[c % SLOTS], y_ss.at[c % SLOTS], y_rs.at[c % SLOTS], device_id=ypeer, device_id_type=MESH
        )

    def copy_x(c):
        return pltpu.make_async_remote_copy(
            x_send.at[c % SLOTS], x_recv.at[c % SLOTS], x_ss.at[c % SLOTS], x_rs.at[c % SLOTS], device_id=xpeer, device_id_type=MESH
        )

    def part_of(k):
        return pl.ds(pl.multiple_of(k * piece, piece), piece)

    def copy_z(c, j):
        return pltpu.make_async_remote_copy(
            z_send.at[c % SLOTS, part_of((z + j) % ZED)], z_recv.at[c % SLOTS, j - 1], z_ss.at[c % SLOTS, j - 1], z_rs.at[c % SLOTS, j - 1],
            device_id=zpeer(j), device_id_type=MESH,
        )

    def copy_w(c, j):
        return pltpu.make_async_remote_copy(
            w_send.at[c % SLOTS], w_recv.at[c % SLOTS, j - 1], w_ss.at[c % SLOTS, j - 1], w_rs.at[c % SLOTS, j - 1],
            device_id=wpeer(j), device_id_type=MESH,
        )

    def copy_g(c, j):
        place = full.at[c, x, part_of(z)]
        return pltpu.make_async_remote_copy(
            place, place, g_ss.at[c % SLOTS, j - 1], g_rs.at[c % SLOTS, j - 1], device_id=zpeer(j), device_id_type=MESH
        )

    def copy_h(c):
        place = full.at[c, x]
        return pltpu.make_async_remote_copy(
            place, place, h_ss.at[c % SLOTS], h_rs.at[c % SLOTS], device_id=xpeer, device_id_type=MESH
        )

    def copy_s(c):
        u, s = c // subs, c % subs
        half = feat // 2
        return [
            pltpu.make_async_copy(
                full.at[c, h],
                sums_hbm.at[
                    pl.ds(pl.multiple_of(s * rows, rows), rows),
                    pl.ds(pl.multiple_of(u * feat + h * half, half), half),
                ],
                s_sem.at[c % STORES, h],
            )
            for h in range(2)
        ]

    def make(c):
        u, s = c // subs, c % subs

        def left_rows(q):
            down = feat * q + quarter * u
            rest = ff + feat * ((u >= 2 * tiles).astype(jnp.int32) + (u > 2 * tiles).astype(jnp.int32)) + quarter * q
            start = jnp.where(u < tiles, down, rest) + s * rows
            return left[pl.ds(pl.multiple_of(start, rows), rows), :]

        order = (2 * (1 - y) + core, 2 * y + core, 2 * (1 - y) + 1 - core, 2 * y + 1 - core)
        lhs = jnp.concatenate([left_rows(q) for q in order], axis=0)
        cols = pl.ds(pl.multiple_of(feat * jnp.maximum(u - tiles + 1, 0), feat), feat)
        total = jnp.dot(lhs, right[:, cols], preferred_element_type=F32)
        slot = c % 2
        own[slot, 0] = total[:rows]
        own[slot, 1] = total[rows : 2 * rows]
        give[slot, 0] = total[2 * rows : 3 * rows].astype(BF16)
        give[slot, 1] = total[3 * rows :].astype(BF16)
        copy_d(c).start()

    def stage_y(c):
        copy_d(c).wait()
        slot = c % 2
        y_send[c % SLOTS] = (own[slot, 0] + d_recv[c % SLOTS, 0].astype(F32)).astype(BF16)
        copy_y(c).start()
        y_keep[c % SLOTS] = own[slot, 1] + d_recv[c % SLOTS, 1].astype(F32)

    def stage_x(c):
        copy_y(c).wait()
        half = feat // 2
        total = y_keep[c % SLOTS] + y_recv[c % SLOTS].astype(F32)

        @pl.when(x == 0)
        def _():
            x_send[c % SLOTS] = total[:, half:].astype(BF16)
            x_keep[c % SLOTS] = total[:, :half]

        @pl.when(x == 1)
        def _():
            x_send[c % SLOTS] = total[:, :half].astype(BF16)
            x_keep[c % SLOTS] = total[:, half:]

        copy_x(c).start()

    def stage_z(c):
        copy_x(c).wait()
        total = x_keep[c % SLOTS] + x_recv[c % SLOTS].astype(F32)
        z_send[c % SLOTS] = total.astype(BF16)
        for j in range(1, ZED):
            copy_z(c, j).start()

    def add_z(c):
        for j in range(1, ZED):
            copy_z(c, j).wait()
        total = z_send[c % SLOTS, part_of(z)].astype(F32)
        for j in range(1, ZED):
            total = total + z_recv[c % SLOTS, j - 1].astype(F32)
        return total

    def stage_w(c):
        w_send[c % SLOTS] = add_z(c).astype(BF16)
        for j in range(1, groups):
            copy_w(c, j).start()

    def add_w(c):
        for j in range(1, groups):
            copy_w(c, j).wait()
        total = w_send[c % SLOTS].astype(F32)
        for j in range(1, groups):
            total = total + w_recv[c % SLOTS, j - 1].astype(F32)
        return total

    def stage_g(c):
        full[c, x, part_of(z)] = (add_z(c) if groups == 1 else add_w(c)).astype(BF16)
        for j in range(1, ZED):
            copy_g(c, j).start()

    def stage_h(c):
        for j in range(1, ZED):
            copy_g(c, j).wait()
        copy_h(c).start()

    def stage_s(c):
        copy_h(c).wait()

        @pl.when(c >= STORES)
        def _():
            for copy in copy_s(c - STORES):
                copy.wait()

        for copy in copy_s(c):
            copy.start()

    ways = [[sib], [ypeer], [xpeer], [zpeer(j) for j in range(1, ZED)]]
    if groups > 1:
        ways.append([wpeer(j) for j in range(1, groups)])
    firsts = [sum(len(way) for way in ways[:i]) for i in range(len(ways))]

    def vector_copies(i):
        return [
            pltpu.make_async_remote_copy(
                vec_sum.at[i], vec_recv.at[firsts[i] + n], v_ss.at[firsts[i] + n], v_rs.at[firsts[i] + n],
                device_id=device, device_id_type=MESH,
            )
            for n, device in enumerate(ways[i])
        ]

    def vector_step(i):
        if i == 0:
            vec_sum[0] = vec_part[...]
        else:
            for copy in vector_copies(i - 1):
                copy.wait()
            total = vec_sum[i - 1]
            for n in range(len(ways[i - 1])):
                total = total + vec_recv[firsts[i - 1] + n]
            vec_sum[i] = total
        if i < len(ways):
            for copy in vector_copies(i):
                copy.start()

    stages = [make, stage_y, stage_x, stage_z] + ([stage_w] if groups > 1 else []) + [stage_g, stage_h, stage_s]
    offsets = [sum(lags[: i + 1]) for i in range(len(stages))]

    def step(t, carry):
        for stage, offset in zip(stages, offsets):
            c = t - offset

            @pl.when((c >= 0) & (c < chunks))
            def _(stage=stage, c=c):
                stage(c)

        return carry

    def run_steps(first, end):
        lax.fori_loop(first, end, step, 0)

    length = len_ref[jnp.maximum(p - 1, 0)]
    keys = lax.broadcasted_iota(jnp.int32, (seq, seq), 0)
    queries = lax.broadcasted_iota(jnp.int32, (seq, seq), 1)
    bias[...] = jnp.where((keys <= queries) & (keys < length), 0.0, -1e30).astype(F32)
    inside = (lax.broadcasted_iota(jnp.int32, (seq, 1), 0) < length).astype(F32)
    low_lanes = lax.broadcasted_iota(jnp.int32, (seq, half), 1) < HEAD

    def pick(values, head):
        zero = jnp.zeros_like(values)
        return jnp.where(low_lanes, values, zero) if head == 0 else jnp.where(low_lanes, zero, values)

    def rows_of(i):
        return pl.ds(i * seq, seq)

    def put_left(offset, i, values):
        left[pl.ds(offset, values.shape[1]), rows_of(i)] = values.T

    N2, CTX, N1 = ff, ff + feat, ff + 2 * feat
    HID, ATT, QKV = feat, feat + ff, 2 * feat + ff

    def forward(i):
        value = state[i]
        n1 = (normalize(value)[0] * row(gain1_ref) + row(shift1_ref)).astype(BF16)
        put_left(N1, i, n1)
        if i == 0:
            weight_copies[0].wait()
        for j in range(3):
            part = dot(n1, wqkv[:, j * feat : (j + 1) * feat])
            if j == 0:
                part = part * HEAD ** (-0.5)
            part = part.astype(BF16)
            qkv[i, :, j * feat : (j + 1) * feat] = part
            if j == 1:
                kt[i] = part.T
            if j == 2:
                vt[i] = part.T

        def group(first_pair, carry):
            mid = seq // 2
            heads = [(u, head) for u in range(FORWARD_PAIRS) for head in range(2)]
            scores = []
            for u, head in heads:
                hp = first_pair * FORWARD_PAIRS + u
                qm = pick(qkv[i, :, pl.ds(pl.multiple_of(hp * half, half), half)], head)
                scores.append([
                    dot_nt(qkv[b, :, pl.ds(pl.multiple_of(feat + hp * half, half), half)], qm)
                    for b in range(i + 1)
                ])
            weights, invs = [], []
            for n, (u, head) in enumerate(heads):
                hp = first_pair * FORWARD_PAIRS + u
                low = [s[:mid, :mid] + bias[:mid, :mid] for s in scores[n]]
                high = [s[:, mid:] + bias[:, mid:] for s in scores[n]]
                parts = []
                stats = []
                for blocks in (low, high):
                    top = functools.reduce(jnp.maximum, [jnp.max(s, axis=0, keepdims=True) for s in blocks])
                    w = [jnp.exp(s - top) for s in blocks]
                    total = sum(jnp.sum(v, axis=0, keepdims=True) for v in w)
                    parts.append([v.astype(BF16) for v in w])
                    stats.append((top, total))
                top = jnp.concatenate([stats[0][0], stats[1][0]], axis=1)
                total = jnp.concatenate([stats[0][1], stats[1][1]], axis=1)
                lse[i, pl.ds(2 * hp + head, 1), :] = top + jnp.log(total)
                zero = jnp.zeros((mid, mid), BF16)
                weights.append([
                    jnp.concatenate([jnp.concatenate([lo, zero], axis=0), hi], axis=1) for lo, hi in zip(*parts)
                ])
                invs.append(1.0 / total)
            for n, (u, head) in enumerate(heads):
                hp = first_pair * FORWARD_PAIRS + u
                rows = pl.ds(pl.multiple_of(hp * half + head * HEAD, HEAD), HEAD)
                acc = sum(dot(vt[b, rows, :], weights[n][b]) for b in range(i + 1)) * invs[n]
                left[pl.ds(pl.multiple_of(CTX + hp * half + head * HEAD, HEAD), HEAD), rows_of(i)] = acc.astype(BF16)
            return carry

        lax.fori_loop(0, feat // half // FORWARD_PAIRS, group, 0)
        ctx[...] = left[pl.ds(CTX, feat), rows_of(i)].T
        if i == 0:
            weight_copies[1].wait()
        mix = state[i] + dot(ctx[...], wout[...])
        mixed[i] = mix
        n2 = (normalize(mix)[0] * row(gain2_ref) + row(shift2_ref)).astype(BF16)
        put_left(N2, i, n2)
        if i == 0:
            weight_copies[2].wait()
            weight_copies[3].wait()
        acc = mix
        for j in range(tiles):
            u = dot(n2, wup[:, j * feat : (j + 1) * feat])
            c = 0.7978845608028654
            square = u * u
            th = jnp.tanh(c * u * (1.0 + 0.044715 * square))
            halfp = 0.5 + 0.5 * th
            active = (u * halfp).astype(BF16)
            slope = halfp + 0.5 * u * (1.0 - th * th) * (c * (1.0 + 3 * 0.044715 * square))
            gp[i, :, j * feat : (j + 1) * feat] = slope.astype(BF16)
            put_left(j * feat, i, active)
            acc = acc + dot(active, wdown[j * feat : (j + 1) * feat, :])
        return acc

    def norm_back(values, d_out, gain, slot, first):
        norm, scale = normalize(values)
        g_gain = jnp.sum(d_out * norm, axis=0, keepdims=True)
        g_shift = jnp.sum(d_out, axis=0, keepdims=True)
        if first:
            vec_part[slot : slot + 1, :] = g_gain
            vec_part[slot + 1 : slot + 2, :] = g_shift
        else:
            vec_part[slot : slot + 1, :] += g_gain
            vec_part[slot + 1 : slot + 2, :] += g_shift
        t = d_out * gain
        return scale * (t - jnp.mean(t, axis=-1, keepdims=True) - norm * jnp.mean(t * norm, axis=-1, keepdims=True))

    def backward(i, grad):
        branch = grad.astype(BF16)
        right[rows_of(i), 0:feat] = branch
        if i == 0:
            run_steps(0, EARLY[0])
        acc = None
        for j in range(tiles):
            d_active = dot_nt(branch, wdown[j * feat : (j + 1) * feat, :])
            d_hidden = (d_active * gp[i, :, j * feat : (j + 1) * feat].astype(F32)).astype(BF16)
            right[rows_of(i), HID + j * feat : HID + (j + 1) * feat] = d_hidden
            term = dot_nt(d_hidden, wup[:, j * feat : (j + 1) * feat])
            acc = term if acc is None else acc + term
        if i == 0:
            run_steps(EARLY[0], EARLY[1])
        d_mixed = grad + norm_back(mixed[i], acc, row(gain2_ref), 2, i == 1)
        d_attn = d_mixed.astype(BF16)
        right[rows_of(i), ATT : ATT + feat] = d_attn
        dctx[...] = dot_nt(d_attn, wout[...]).astype(BF16)

        def group(first_pair, carry):
            mid = seq // 2
            for u in range(BACKWARD_PAIRS):
                hp = first_pair * BACKWARD_PAIRS + u
                lanes = pl.ds(pl.multiple_of(hp * half, half), half)
                q2 = qkv[i, :, lanes]
                do2 = dctx[:, lanes]
                dk = [None] * (i + 1)
                dv = [None] * (i + 1)
                zero = jnp.zeros((mid, mid), BF16)
                for head in range(2):
                    qm = pick(q2, head)
                    dom = pick(do2, head)
                    lrow = lse[i, pl.ds(2 * hp + head, 1), :]
                    soft = [[], []]
                    d_soft = [[], []]
                    for b in range(i + 1):
                        k2 = qkv[b, :, pl.ds(pl.multiple_of(feat + hp * half, half), half)]
                        v2 = qkv[b, :, pl.ds(pl.multiple_of(2 * feat + hp * half, half), half)]
                        s = dot_nt(k2, qm)
                        d = dot_nt(v2, dom)
                        soft[0].append(jnp.exp(s[:mid, :mid] + (bias[:mid, :mid] - lrow[:, :mid])))
                        soft[1].append(jnp.exp(s[:, mid:] + (bias[:, mid:] - lrow[:, mid:])))
                        d_soft[0].append(d[:mid, :mid])
                        d_soft[1].append(d[:, mid:])
                    inner = [
                        sum(jnp.sum(a * c, axis=0, keepdims=True) for a, c in zip(soft[h], d_soft[h])) for h in range(2)
                    ]
                    rows = pl.ds(pl.multiple_of(hp * half + head * HEAD, HEAD), HEAD)
                    dq = None

                    def whole(lo, hi):
                        return jnp.concatenate([jnp.concatenate([lo, zero], axis=0), hi], axis=1)

                    for b in range(i + 1):
                        d_score = whole(*[(soft[h][b] * (d_soft[h][b] - inner[h])).astype(BF16) for h in range(2)])
                        prob = whole(*[soft[h][b].astype(BF16) for h in range(2)])
                        term_v = dot(prob, dom)
                        term_k = dot(d_score, qm)
                        term_q = dot(kt[b, rows, :], d_score)
                        dv[b] = term_v if dv[b] is None else dv[b] + term_v
                        dk[b] = term_k if dk[b] is None else dk[b] + term_k
                        dq = term_q if dq is None else dq + term_q
                    dqt[rows, :] = (dq * HEAD ** (-0.5)).astype(BF16)
                dk_own, dv_own = dk[i], dv[i]
                if i == 1:
                    dk_more[:, lanes] = dk[0]
                    dv_more[:, lanes] = dv[0]
                else:
                    dk_own = dk_own + dk_more[:, lanes]
                    dv_own = dv_own + dv_more[:, lanes]
                right[rows_of(i), pl.ds(pl.multiple_of(QKV + feat + hp * half, half), half)] = dk_own.astype(BF16)
                right[rows_of(i), pl.ds(pl.multiple_of(QKV + 2 * feat + hp * half, half), half)] = dv_own.astype(BF16)
            if i == 0:
                step(EARLY[1] + first_pair, 0)
            return carry

        lax.fori_loop(0, feat // half // BACKWARD_PAIRS, group, 0)
        right[rows_of(i), QKV : QKV + feat] = dqt[...].T
        d_normed = None
        for j in range(3):
            term = dot_nt(
                right[rows_of(i), QKV + j * feat : QKV + (j + 1) * feat], wqkv[:, j * feat : (j + 1) * feat]
            )
            d_normed = term if d_normed is None else d_normed + term
        return d_mixed + norm_back(state[i], d_normed, row(gain1_ref), 0, i == 1)

    wait_inputs(0)
    state[0] = x_ref[...].astype(F32)
    first = forward(0)
    state[1] = first.astype(BF16).astype(F32) + row(embed_ref)
    second = forward(1)
    out_seq[...] = (second * inside).astype(BF16)
    wait_inputs(1)

    def send_results(n):
        @pl.when(p > 0)
        def _():
            for j in range(1, size):
                result_copies(j)[n].start()
            own_results()[n].start()

    send_results(0)
    d_carry = backward(1, cot_ref[...].astype(F32) * inside)
    vec_part[4:5, :] = jnp.sum(d_carry, axis=0, keepdims=True)
    vec_part[5:8, :] = jnp.zeros((3, feat), F32)
    d_state = backward(0, d_carry.astype(BF16).astype(F32))
    grad_seq[...] = d_state.astype(BF16)
    send_results(1)

    begun = EARLY[1] + feat // half // BACKWARD_PAIRS
    vector_step(0)

    def late_step(t, carry):
        step(t, 0)
        for i in range(1, len(ways) + 1):
            @pl.when(t == begun + 3 * i)
            def _(i=i):
                vector_step(i)

        return carry

    lax.fori_loop(begun, chunks + offsets[-1], late_step, 0)
    vec_ref[...] = vec_sum[len(ways)]

    @pl.when(p > 0)
    def _():
        for copy in own_results():
            copy.wait()
        for j in range(1, size):
            for copy in result_copies(j):
                copy.wait_send()

    for j in range(1, size):
        source = (p + size - j) % size

        @pl.when(source > 0)
        def _(j=j, source=source):
            for n, dst in enumerate((out_ref, gin_ref)):
                pltpu.make_async_copy(dst.at[source - 1], dst.at[source - 1], o_rs.at[n, j - 1]).wait()

    def finish(c, carry):
        for copy in copy_s(c):
            copy.wait()
        return carry

    lax.fori_loop(chunks - STORES, chunks, finish, 0)


def run_block(inputs, cotangent, lengths, vectors, w_qkv, w_out, w_up, w_down, rows, lags, groups):
    slots, block, feat = inputs.shape
    ff = w_up.shape[1]
    seq = (slots + 1) * block
    quarter = feat // 4
    units = (2 * ff + 4 * feat) // feat
    chunks = units * (quarter // rows)
    piece = rows // ZED
    half = feat // 2
    ways = 4 + (groups > 1)
    landings = 6 + (groups - 1)
    more = max(groups - 1, 1)
    dma = pltpu.SemaphoreType.DMA
    local_block = jax.ShapeDtypeStruct((slots, block, feat), BF16)
    left_rows = ff + 3 * feat
    right_cols = 5 * feat + ff
    return pl.pallas_call(
        functools.partial(block_kernel, (rows, lags, groups)),
        out_shape=(
            jax.ShapeDtypeStruct((quarter, units * feat), BF16),
            local_block,
            local_block,
            jax.ShapeDtypeStruct((8, feat), F32),
        ),
        in_specs=[VMEM, VMEM, SMEM] + [VMEM] * 5 + [ANY] * 4,
        out_specs=(ANY, VMEM, VMEM, VMEM),
        scratch_shapes=[
            pltpu.VMEM((seq, feat), BF16),
            pltpu.VMEM((seq, feat), BF16),
            pltpu.VMEM((seq, feat), BF16),
            pltpu.VMEM((seq, feat), BF16),
            pltpu.VMEM((8, feat), F32),
            pltpu.VMEM((ways + 1, 8, feat), F32),
            pltpu.VMEM(w_qkv.shape, BF16),
            pltpu.VMEM(w_out.shape, BF16),
            pltpu.VMEM(w_up.shape, BF16),
            pltpu.VMEM(w_down.shape, BF16),
            pltpu.VMEM((left_rows, 2 * seq), BF16),
            pltpu.VMEM((2 * seq, right_cols), BF16),
            pltpu.VMEM((2, seq, 3 * feat), BF16),
            pltpu.VMEM((2, feat, seq), BF16),
            pltpu.VMEM((2, feat, seq), BF16),
            pltpu.VMEM((2, 16, seq), F32),
            pltpu.VMEM((2, seq, ff), BF16),
            pltpu.VMEM((2, seq, feat), F32),
            pltpu.VMEM((2, seq, feat), F32),
            pltpu.VMEM((seq, feat), BF16),
            pltpu.VMEM((seq, feat), F32),
            pltpu.VMEM((seq, feat), F32),
            pltpu.VMEM((feat, seq), BF16),
            pltpu.VMEM((seq, feat), BF16),
            pltpu.VMEM((seq, seq), F32),
            pltpu.VMEM((2, 2, rows, feat), F32),
            pltpu.VMEM((2, 2, rows, feat), BF16),
            pltpu.VMEM((SLOTS, 2, rows, feat), BF16),
            pltpu.VMEM((SLOTS, rows, feat), BF16),
            pltpu.VMEM((SLOTS, rows, feat), F32),
            pltpu.VMEM((SLOTS, rows, feat), BF16),
            pltpu.VMEM((SLOTS, rows, half), BF16),
            pltpu.VMEM((SLOTS, rows, half), F32),
            pltpu.VMEM((SLOTS, rows, half), BF16),
            pltpu.VMEM((SLOTS, rows, half), BF16),
            pltpu.VMEM((SLOTS, ZED - 1, piece, half), BF16),
            pltpu.VMEM((SLOTS if groups > 1 else 1, piece, half), BF16),
            pltpu.VMEM((SLOTS if groups > 1 else 1, more, piece, half), BF16),
            pltpu.VMEM((chunks, 2, rows, half), BF16),
            pltpu.VMEM((landings, 8, feat), F32),
            dma((4,)), dma((2, slots)), dma((2, slots)),
            dma((SLOTS,)), dma((SLOTS,)), dma((SLOTS,)), dma((SLOTS,)), dma((SLOTS,)), dma((SLOTS,)),
            dma((SLOTS, ZED - 1)), dma((SLOTS, ZED - 1)),
            dma((SLOTS if groups > 1 else 1, more)), dma((SLOTS if groups > 1 else 1, more)),
            dma((SLOTS, ZED - 1)), dma((SLOTS, ZED - 1)),
            dma((SLOTS,)), dma((SLOTS,)), dma((STORES, 2)),
            dma((2, slots)), dma((2, slots)), dma((landings,)), dma((landings,)), dma((2,)),
        ],
        compiler_params=pltpu.CompilerParams(
            collective_id=0, has_side_effects=True, vmem_limit_bytes=60 * 2**20
        ),
    )(inputs, cotangent, lengths, *vectors, w_qkv, w_out, w_up, w_down)


def finish_kernel(
    sums_hbm, block_ref, grads_ref, vec_ref,
    block_out, grads_out, qkv_out, out_out, up_out, down_out, gain1_out, shift1_out, gain2_out, shift2_out, embed_out,
    low, high, l_sem, s_sem, c_sem,
):
    feat = vec_ref.shape[1]
    quarter = feat // 4
    units, tiles = low.shape[0], up_out.shape[1] // feat
    passed = [
        pltpu.make_async_copy(block_ref, block_out, c_sem.at[0]),
        pltpu.make_async_copy(grads_ref, grads_out, c_sem.at[1]),
    ]
    loads = [
        pltpu.make_async_copy(sums_hbm.at[:, pl.ds(u * feat, feat)], low.at[u], l_sem.at[u]) for u in range(units)
    ]
    for copy in loads + passed:
        copy.start()
    vec = pltpu.roll(vec_ref[...], feat - quarter * lax.axis_index("pipe"), 1)
    for n, ref in enumerate((gain1_out, shift1_out, gain2_out, shift2_out, embed_out)):
        ref[...] = vec[n, :quarter]
    stores = []
    for u in range(units):
        loads[u].wait()
        high[u] = low[u].astype(F32)
        if u < tiles:
            place = down_out.at[pl.ds(u * quarter, quarter)]
        elif u < 2 * tiles:
            place = up_out.at[:, pl.ds((u - tiles) * feat, feat)]
        elif u == 2 * tiles:
            place = out_out
        else:
            place = qkv_out.at[:, pl.ds((u - 2 * tiles - 1) * feat, feat)]
        copy = pltpu.make_async_copy(high.at[u], place, s_sem.at[u])
        copy.start()
        stores.append(copy)
    for copy in stores + passed:
        copy.wait()


def run_finish(sums, block_out, input_grads, vec, ff):
    feat = vec.shape[1]
    quarter = feat // 4
    units = sums.shape[1] // feat
    dma = pltpu.SemaphoreType.DMA

    def result(*shape):
        return jax.ShapeDtypeStruct(shape, F32)

    return pl.pallas_call(
        finish_kernel,
        out_shape=(
            jax.ShapeDtypeStruct(block_out.shape, BF16),
            jax.ShapeDtypeStruct(input_grads.shape, BF16),
            result(quarter, 3 * feat), result(quarter, feat), result(quarter, ff), result(ff // 4, feat),
        ) + (result(quarter),) * 5,
        in_specs=[ANY, VMEM, VMEM, VMEM],
        out_specs=(ANY,) * 6 + (VMEM,) * 5,
        scratch_shapes=[
            pltpu.VMEM((units, quarter, feat), BF16),
            pltpu.VMEM((units, quarter, feat), F32),
            dma((units,)), dma((units,)), dma((2,)),
        ],
        compiler_params=pltpu.CompilerParams(vmem_limit_bytes=60 * 2**20),
    )(sums, block_out, input_grads, vec)


def shards(
    inputs, lengths, w_qkv, w_out, w_up, w_down, norm1_gain, norm1_shift, norm2_gain, norm2_shift, pass_embed, cotangent
):
    ff = w_up.shape[1]
    groups = lax.axis_size("dp") // (2 * ZED)
    vectors = (norm1_gain, norm1_shift, norm2_gain, norm2_shift, pass_embed)
    sums, block_out, input_grads, vec = run_block(
        inputs, cotangent, lengths, vectors, w_qkv, w_out, w_up, w_down, ROWS, LAGS[: 7 + (groups > 1)], groups
    )
    return run_finish(sums, block_out, input_grads, vec, ff)


def solution(mesh):
    rep = P()
    seqs = P("dp", "pipe", None)
    return jax.shard_map(
        shards,
        mesh=mesh,
        in_specs=(seqs, P("dp")) + (rep,) * 9 + (seqs,),
        out_specs=(seqs, seqs) + (P("pipe", None),) * 4 + (P("pipe"),) * 5,
        check_vma=False,
    )
```

```python
import functools

import jax
import jax.numpy as jnp
from jax import lax
from jax.experimental import pallas as pl
from jax.experimental.pallas import tpu as pltpu
from jax.sharding import PartitionSpec as P

MESH = pl.DeviceIdType.MESH
HEADS = 12
HEAD = 64
F32 = jnp.float32
BF16 = jnp.bfloat16
ANY = pl.BlockSpec(memory_space=pl.ANY)
VMEM = pl.BlockSpec(memory_space=pltpu.VMEM)
SMEM = pl.BlockSpec(memory_space=pltpu.SMEM)


def dot(left, right):
    return jnp.dot(left, right, preferred_element_type=F32)


def dot_nt(left, right):
    return lax.dot_general(left, right, (((1,), (1,)), ((), ())), preferred_element_type=F32)


def row(ref):
    return ref[...].reshape(1, ref.shape[0])


def normalize(values):
    center = values - jnp.mean(values, axis=-1, keepdims=True)
    scale = lax.rsqrt(jnp.mean(center * center, axis=-1, keepdims=True) + 1e-05)
    return center * scale, scale


ZED = 4
SLOTS = 8
ROWS = 64
LAGS = (0, 1, 2, 2, 2, 2, 2, 2)
EARLY = (3, 6)
FORWARD_PAIRS = 6
BACKWARD_PAIRS = (1, 6)


def block_kernel(
    dims, in_hbm, given_hbm, len_ref, gain1_ref, shift1_ref, gain2_ref, shift2_ref, embed_ref,
    wqkv_hbm, wout_hbm, wup_hbm, wdown_hbm,
    sums_hbm, out_ref, gin_ref, vec_ref,
    in_ref, given_ref, x_ref, cot_ref, out_seq, grad_seq, vec_part, vec_sum,
    wqkv, wout, wup, wdown, left, right, qkv, vt, kt, lse, gp, mixed, state, ctx,
    dk_more, dv_more, dqt, dctx, bias,
    own, give, d_recv, y_send, y_keep, y_recv, x_send, x_keep, x_recv,
    z_send, z_recv, w_send, w_recv, full, vec_recv,
    a_sem, w_sem, i_ss, i_rs, d_ss, d_rs, y_ss, y_rs, x_ss, x_rs, z_ss, z_rs, w_ss, w_rs, g_ss, g_rs, h_ss, h_rs, s_sem,
    o_ss, o_rs, v_ss, v_rs, local,
):
    rows, lags, groups = dims
    slots, block, feat = in_hbm.shape
    size = slots + 1
    seq = size * block
    ff = wup.shape[1]
    tiles = ff // feat
    half = feat // 6
    units = (2 * ff + 4 * feat) // feat
    quarter = feat // 4
    subs = quarter // rows
    chunks = units * subs
    piece = rows // ZED
    g = lax.axis_index("dp")
    p = lax.axis_index("pipe")
    core, y = p % 2, p // 2
    x, z, w = g % 2, (g // 2) % ZED, g // (2 * ZED)
    sib = (g, p + 1 - 2 * core)
    ypeer = (g, p + 2 - 4 * y)
    diag = (g, 3 - p)
    xpeer = (g + 1 - 2 * x, p)

    def zpeer(j):
        return (g + 2 * ((z + j) % ZED - z), p)

    def wpeer(j):
        return (g + 2 * ZED * ((w + j) % groups - w), p)

    def zflip(step):
        return (2 * ZED * w + 2 * (z + step * (1 - 2 * ((z // step) % 2))) + x, p)

    everyone = [sib, ypeer, diag, xpeer] + [zpeer(j) for j in range(1, ZED)] + [wpeer(j) for j in range(1, groups)]

    arrivals = [
        pltpu.make_async_copy(in_hbm, in_ref, a_sem.at[0]),
        pltpu.make_async_copy(given_hbm, given_ref, a_sem.at[1]),
    ]
    for copy in arrivals:
        copy.start()
    weight_copies = [
        pltpu.make_async_copy(src, dst, w_sem.at[i])
        for i, (src, dst) in enumerate(
            ((wqkv_hbm, wqkv), (wout_hbm, wout), (wup_hbm, wup), (wdown_hbm, wdown))
        )
    ]
    for copy in weight_copies:
        copy.start()

    barrier = pltpu.get_barrier_semaphore()
    for device in everyone:
        pl.semaphore_signal(barrier, inc=1, device_id=device, device_id_type=MESH)
    pl.semaphore_wait(barrier, len(everyone))

    mine = pl.ds(pl.multiple_of(p * block, block), block)

    def input_copies(j):
        peer = (p + j) % size
        slot = jnp.maximum(peer - 1, 0)
        return [
            pltpu.make_async_remote_copy(
                src.at[slot], dst.at[mine], i_ss.at[n, j - 1], i_rs.at[n, j - 1],
                device_id=(g, peer), device_id_type=MESH,
            )
            for n, (src, dst) in enumerate(((in_ref, x_ref), (given_ref, cot_ref)))
        ]

    def own_inputs():
        slot = jnp.maximum(p - 1, 0)
        return [
            pltpu.make_async_copy(src.at[slot], dst.at[mine], local.at[n])
            for n, (src, dst) in enumerate(((in_ref, x_ref), (given_ref, cot_ref)))
        ]

    def wait_inputs(n):
        @pl.when(p > 0)
        def _():
            own_inputs()[n].wait()
            for j in range(1, size):
                input_copies(j)[n].wait_recv()

        for j in range(1, size):
            @pl.when((p + j) % size > 0)
            def _(j=j):
                input_copies(j)[n].wait_send()

    def send_inputs(n):
        for j in range(1, size):
            @pl.when((p + j) % size > 0)
            def _(j=j):
                input_copies(j)[n].start()

        @pl.when(p > 0)
        def _():
            own_inputs()[n].start()

    arrivals[0].wait()
    send_inputs(0)

    @pl.when(p == 0)
    def _():
        x_ref[...] = jnp.zeros(x_ref.shape, x_ref.dtype)
        cot_ref[...] = jnp.zeros(cot_ref.shape, cot_ref.dtype)

    slots, block, _ = out_ref.shape
    size = slots + 1

    def result_copies(j):
        peer = (p + j) % size
        slot = jnp.maximum(p - 1, 0)
        part = pl.ds(pl.multiple_of(peer * block, block), block)
        return [
            pltpu.make_async_remote_copy(
                src.at[part], dst.at[slot], o_ss.at[n, j - 1], o_rs.at[n, j - 1],
                device_id=(g, peer), device_id_type=MESH,
            )
            for n, (src, dst) in enumerate(((out_seq, out_ref), (grad_seq, gin_ref)))
        ]

    def own_results():
        part = pl.ds(pl.multiple_of(p * block, block), block)
        slot = jnp.maximum(p - 1, 0)
        return [
            pltpu.make_async_copy(out_seq.at[part], out_ref.at[slot], local.at[0]),
            pltpu.make_async_copy(grad_seq.at[part], gin_ref.at[slot], local.at[1]),
        ]

    def copy_d(c):
        return pltpu.make_async_remote_copy(
            give.at[c % 2], d_recv.at[c % SLOTS], d_ss.at[c % SLOTS], d_rs.at[c % SLOTS], device_id=sib, device_id_type=MESH
        )

    def copy_y(c):
        return pltpu.make_async_remote_copy(
            y_send.at[c % SLOTS], y_recv.at[c % SLOTS], y_ss.at[c % SLOTS], y_rs.at[c % SLOTS], device_id=ypeer, device_id_type=MESH
        )

    def copy_x(c):
        return pltpu.make_async_remote_copy(
            x_send.at[c % SLOTS], x_recv.at[c % SLOTS], x_ss.at[c % SLOTS], x_rs.at[c % SLOTS], device_id=xpeer, device_id_type=MESH
        )

    def part_of(k):
        return pl.ds(pl.multiple_of(k * piece, piece), piece)

    def copy_z(c, j):
        return pltpu.make_async_remote_copy(
            z_send.at[c % SLOTS, part_of((z + j) % ZED)], z_recv.at[c % SLOTS, j - 1], z_ss.at[c % SLOTS, j - 1], z_rs.at[c % SLOTS, j - 1],
            device_id=zpeer(j), device_id_type=MESH,
        )

    def copy_w(c, j):
        return pltpu.make_async_remote_copy(
            w_send.at[c % SLOTS], w_recv.at[c % SLOTS, j - 1], w_ss.at[c % SLOTS, j - 1], w_rs.at[c % SLOTS, j - 1],
            device_id=wpeer(j), device_id_type=MESH,
        )

    def copy_g(c, j):
        place = full.at[c, x, part_of(z)]
        return pltpu.make_async_remote_copy(
            place, place, g_ss.at[c % SLOTS, j - 1], g_rs.at[c % SLOTS, j - 1], device_id=zpeer(j), device_id_type=MESH
        )

    def copy_h(c):
        place = full.at[c, x]
        return pltpu.make_async_remote_copy(
            place, place, h_ss.at[c % SLOTS], h_rs.at[c % SLOTS], device_id=xpeer, device_id_type=MESH
        )

    def copy_s(c):
        u, s = c // subs, c % subs
        half = feat // 2
        return [
            pltpu.make_async_copy(
                full.at[c, h],
                sums_hbm.at[
                    pl.ds(pl.multiple_of(s * rows, rows), rows),
                    pl.ds(pl.multiple_of(u * feat + h * half, half), half),
                ],
                s_sem.at[h],
            )
            for h in range(2)
        ]

    def make(c):
        u, s = c // subs, c % subs

        def left_rows(q):
            down = feat * q + quarter * u
            rest = ff + feat * ((u >= 2 * tiles).astype(jnp.int32) + (u > 2 * tiles).astype(jnp.int32)) + quarter * q
            start = jnp.where(u < tiles, down, rest) + s * rows
            return left[pl.ds(pl.multiple_of(start, rows), rows), :]

        order = (2 * (1 - y) + core, 2 * y + core, 2 * (1 - y) + 1 - core, 2 * y + 1 - core)
        lhs = jnp.concatenate([left_rows(q) for q in order], axis=0)
        cols = pl.ds(pl.multiple_of(feat * jnp.maximum(u - tiles + 1, 0), feat), feat)
        total = jnp.dot(lhs, right[:, cols], preferred_element_type=F32)
        slot = c % 2
        own[slot, 0] = total[:rows]
        own[slot, 1] = total[rows : 2 * rows]
        give[slot, 0] = total[2 * rows : 3 * rows].astype(BF16)
        give[slot, 1] = total[3 * rows :].astype(BF16)
        copy_d(c).start()

    def stage_y(c):
        copy_d(c).wait()
        slot = c % 2
        y_send[c % SLOTS] = (own[slot, 0] + d_recv[c % SLOTS, 0].astype(F32)).astype(BF16)
        copy_y(c).start()
        y_keep[c % SLOTS] = own[slot, 1] + d_recv[c % SLOTS, 1].astype(F32)

    def stage_x(c):
        copy_y(c).wait()
        half = feat // 2
        total = y_keep[c % SLOTS] + y_recv[c % SLOTS].astype(F32)

        @pl.when(x == 0)
        def _():
            x_send[c % SLOTS] = total[:, half:].astype(BF16)
            x_keep[c % SLOTS] = total[:, :half]

        @pl.when(x == 1)
        def _():
            x_send[c % SLOTS] = total[:, :half].astype(BF16)
            x_keep[c % SLOTS] = total[:, half:]

        copy_x(c).start()

    def stage_z(c):
        copy_x(c).wait()
        total = x_keep[c % SLOTS] + x_recv[c % SLOTS].astype(F32)
        z_send[c % SLOTS] = total.astype(BF16)
        for j in range(1, ZED):
            copy_z(c, j).start()

    def add_z(c):
        for j in range(1, ZED):
            copy_z(c, j).wait()
        total = z_send[c % SLOTS, part_of(z)].astype(F32)
        for j in range(1, ZED):
            total = total + z_recv[c % SLOTS, j - 1].astype(F32)
        return total

    def stage_w(c):
        w_send[c % SLOTS] = add_z(c).astype(BF16)
        for j in range(1, groups):
            copy_w(c, j).start()

    def add_w(c):
        for j in range(1, groups):
            copy_w(c, j).wait()
        total = w_send[c % SLOTS].astype(F32)
        for j in range(1, groups):
            total = total + w_recv[c % SLOTS, j - 1].astype(F32)
        return total

    def stage_g(c):
        full[c, x, part_of(z)] = (add_z(c) if groups == 1 else add_w(c)).astype(BF16)
        for j in range(1, ZED):
            copy_g(c, j).start()

    def stage_h(c):
        for j in range(1, ZED):
            copy_g(c, j).wait()
        copy_h(c).start()

    def stage_s(c):
        copy_h(c).wait()
        for copy in copy_s(c):
            copy.start()

    ways = [[sib], [ypeer], [xpeer], [zflip(1)], [zflip(2)]]
    if groups > 1:
        ways.append([wpeer(j) for j in range(1, groups)])
    firsts = [sum(len(way) for way in ways[:i]) for i in range(len(ways))]

    def vector_copies(i):
        return [
            pltpu.make_async_remote_copy(
                vec_sum.at[i], vec_recv.at[firsts[i] + n], v_ss.at[firsts[i] + n], v_rs.at[firsts[i] + n],
                device_id=device, device_id_type=MESH,
            )
            for n, device in enumerate(ways[i])
        ]

    def vector_step(i):
        if i == 0:
            vec_sum[0] = vec_part[...]
        else:
            for copy in vector_copies(i - 1):
                copy.wait()
            total = vec_sum[i - 1]
            for n in range(len(ways[i - 1])):
                total = total + vec_recv[firsts[i - 1] + n]
            vec_sum[i] = total
        if i < len(ways):
            for copy in vector_copies(i):
                copy.start()

    stages = [make, stage_y, stage_x, stage_z] + ([stage_w] if groups > 1 else []) + [stage_g, stage_h, stage_s]
    offsets = [sum(lags[: i + 1]) for i in range(len(stages))]

    def step(t, carry):
        for stage, offset in zip(stages, offsets):
            c = t - offset

            @pl.when((c >= 0) & (c < chunks))
            def _(stage=stage, c=c):
                stage(c)

        return carry

    def run_steps(first, end):
        lax.fori_loop(first, end, step, 0)

    length = len_ref[jnp.maximum(p - 1, 0)]
    keys = lax.broadcasted_iota(jnp.int32, (seq, seq), 0)
    queries = lax.broadcasted_iota(jnp.int32, (seq, seq), 1)
    bias[...] = jnp.where((keys <= queries) & (keys < length), 0.0, -1e30).astype(F32)
    inside = (lax.broadcasted_iota(jnp.int32, (seq, 1), 0) < length).astype(F32)
    low_lanes = lax.broadcasted_iota(jnp.int32, (seq, half), 1) < HEAD

    def pick(values, head):
        zero = jnp.zeros_like(values)
        return jnp.where(low_lanes, values, zero) if head == 0 else jnp.where(low_lanes, zero, values)

    def rows_of(i):
        return pl.ds(i * seq, seq)

    def put_left(offset, i, values):
        left[pl.ds(offset, values.shape[1]), rows_of(i)] = values.T

    N2, CTX, N1 = ff, ff + feat, ff + 2 * feat
    HID, ATT, QKV = feat, feat + ff, 2 * feat + ff

    def forward(i):
        value = state[i]
        n1 = (normalize(value)[0] * row(gain1_ref) + row(shift1_ref)).astype(BF16)
        put_left(N1, i, n1)
        if i == 0:
            weight_copies[0].wait()
        for j in range(3):
            part = dot(n1, wqkv[:, j * feat : (j + 1) * feat])
            if j == 0:
                part = part * HEAD ** (-0.5)
            part = part.astype(BF16)
            qkv[i, :, j * feat : (j + 1) * feat] = part
            if j == 1:
                kt[i] = part.T
            if j == 2:
                vt[i] = part.T

        def group(first_pair, carry):
            mid = seq // 2
            heads = [(u, head) for u in range(FORWARD_PAIRS) for head in range(2)]
            scores = []
            for u, head in heads:
                hp = first_pair * FORWARD_PAIRS + u
                qm = pick(qkv[i, :, pl.ds(pl.multiple_of(hp * half, half), half)], head)
                scores.append([
                    dot_nt(qkv[b, :, pl.ds(pl.multiple_of(feat + hp * half, half), half)], qm)
                    for b in range(i + 1)
                ])
            weights, invs = [], []
            for n, (u, head) in enumerate(heads):
                hp = first_pair * FORWARD_PAIRS + u
                low = [s[:mid, :mid] + bias[:mid, :mid] for s in scores[n]]
                high = [s[:, mid:] + bias[:, mid:] for s in scores[n]]
                parts = []
                stats = []
                for blocks in (low, high):
                    top = functools.reduce(jnp.maximum, [jnp.max(s, axis=0, keepdims=True) for s in blocks])
                    w = [jnp.exp(s - top) for s in blocks]
                    total = sum(jnp.sum(v, axis=0, keepdims=True) for v in w)
                    parts.append([v.astype(BF16) for v in w])
                    stats.append((top, total))
                top = jnp.concatenate([stats[0][0], stats[1][0]], axis=1)
                total = jnp.concatenate([stats[0][1], stats[1][1]], axis=1)
                lse[i, pl.ds(2 * hp + head, 1), :] = top + jnp.log(total)
                zero = jnp.zeros((mid, mid), BF16)
                weights.append([
                    jnp.concatenate([jnp.concatenate([lo, zero], axis=0), hi], axis=1) for lo, hi in zip(*parts)
                ])
                invs.append(1.0 / total)
            for n, (u, head) in enumerate(heads):
                hp = first_pair * FORWARD_PAIRS + u
                rows = pl.ds(pl.multiple_of(hp * half + head * HEAD, HEAD), HEAD)
                acc = sum(dot(vt[b, rows, :], weights[n][b]) for b in range(i + 1)) * invs[n]
                left[pl.ds(pl.multiple_of(CTX + hp * half + head * HEAD, HEAD), HEAD), rows_of(i)] = acc.astype(BF16)
            return carry

        lax.fori_loop(0, feat // half // FORWARD_PAIRS, group, 0)
        ctx[...] = left[pl.ds(CTX, feat), rows_of(i)].T
        if i == 0:
            weight_copies[1].wait()
        mix = state[i] + dot(ctx[...], wout[...])
        mixed[i] = mix
        n2 = (normalize(mix)[0] * row(gain2_ref) + row(shift2_ref)).astype(BF16)
        put_left(N2, i, n2)
        if i == 0:
            weight_copies[2].wait()
            weight_copies[3].wait()
        acc = mix
        for j in range(tiles):
            u = dot(n2, wup[:, j * feat : (j + 1) * feat])
            c = 0.7978845608028654
            square = u * u
            th = jnp.tanh(c * u * (1.0 + 0.044715 * square))
            halfp = 0.5 + 0.5 * th
            active = (u * halfp).astype(BF16)
            slope = halfp + 0.5 * u * (1.0 - th * th) * (c * (1.0 + 3 * 0.044715 * square))
            gp[i, :, j * feat : (j + 1) * feat] = slope.astype(BF16)
            put_left(j * feat, i, active)
            acc = acc + dot(active, wdown[j * feat : (j + 1) * feat, :])
        return acc

    def norm_back(values, d_out, gain, slot, first):
        norm, scale = normalize(values)
        g_gain = jnp.sum(d_out * norm, axis=0, keepdims=True)
        g_shift = jnp.sum(d_out, axis=0, keepdims=True)
        if first:
            vec_part[slot : slot + 1, :] = g_gain
            vec_part[slot + 1 : slot + 2, :] = g_shift
        else:
            vec_part[slot : slot + 1, :] += g_gain
            vec_part[slot + 1 : slot + 2, :] += g_shift
        t = d_out * gain
        return scale * (t - jnp.mean(t, axis=-1, keepdims=True) - norm * jnp.mean(t * norm, axis=-1, keepdims=True))

    def backward(i, grad):
        pairs = BACKWARD_PAIRS[i]
        branch = grad.astype(BF16)
        right[rows_of(i), 0:feat] = branch
        if i == 0:
            run_steps(0, EARLY[0])
        acc = None
        for j in range(tiles):
            d_active = dot_nt(branch, wdown[j * feat : (j + 1) * feat, :])
            d_hidden = (d_active * gp[i, :, j * feat : (j + 1) * feat].astype(F32)).astype(BF16)
            right[rows_of(i), HID + j * feat : HID + (j + 1) * feat] = d_hidden
            term = dot_nt(d_hidden, wup[:, j * feat : (j + 1) * feat])
            acc = term if acc is None else acc + term
        if i == 0:
            run_steps(EARLY[0], EARLY[1])
        d_mixed = grad + norm_back(mixed[i], acc, row(gain2_ref), 2, i == 1)
        d_attn = d_mixed.astype(BF16)
        right[rows_of(i), ATT : ATT + feat] = d_attn
        dctx[...] = dot_nt(d_attn, wout[...]).astype(BF16)

        def group(first_pair, carry):
            mid = seq // 2
            for u in range(pairs):
                hp = first_pair * pairs + u
                lanes = pl.ds(pl.multiple_of(hp * half, half), half)
                q2 = qkv[i, :, lanes]
                do2 = dctx[:, lanes]
                dk = [None] * (i + 1)
                dv = [None] * (i + 1)
                zero = jnp.zeros((mid, mid), BF16)
                for head in range(2):
                    qm = pick(q2, head)
                    dom = pick(do2, head)
                    lrow = lse[i, pl.ds(2 * hp + head, 1), :]
                    soft = [[], []]
                    d_soft = [[], []]
                    for b in range(i + 1):
                        k2 = qkv[b, :, pl.ds(pl.multiple_of(feat + hp * half, half), half)]
                        v2 = qkv[b, :, pl.ds(pl.multiple_of(2 * feat + hp * half, half), half)]
                        s = dot_nt(k2, qm)
                        d = dot_nt(v2, dom)
                        soft[0].append(jnp.exp(s[:mid, :mid] + (bias[:mid, :mid] - lrow[:, :mid])))
                        soft[1].append(jnp.exp(s[:, mid:] + (bias[:, mid:] - lrow[:, mid:])))
                        d_soft[0].append(d[:mid, :mid])
                        d_soft[1].append(d[:, mid:])
                    inner = [
                        sum(jnp.sum(a * c, axis=0, keepdims=True) for a, c in zip(soft[h], d_soft[h])) for h in range(2)
                    ]
                    rows = pl.ds(pl.multiple_of(hp * half + head * HEAD, HEAD), HEAD)
                    dq = None

                    def whole(lo, hi):
                        return jnp.concatenate([jnp.concatenate([lo, zero], axis=0), hi], axis=1)

                    for b in range(i + 1):
                        d_score = whole(*[(soft[h][b] * (d_soft[h][b] - inner[h])).astype(BF16) for h in range(2)])
                        prob = whole(*[soft[h][b].astype(BF16) for h in range(2)])
                        term_v = dot(prob, dom)
                        term_k = dot(d_score, qm)
                        term_q = dot(kt[b, rows, :], d_score)
                        dv[b] = term_v if dv[b] is None else dv[b] + term_v
                        dk[b] = term_k if dk[b] is None else dk[b] + term_k
                        dq = term_q if dq is None else dq + term_q
                    dqt[rows, :] = (dq * HEAD ** (-0.5)).astype(BF16)
                dk_own, dv_own = dk[i], dv[i]
                if i == 1:
                    dk_more[:, lanes] = dk[0]
                    dv_more[:, lanes] = dv[0]
                else:
                    dk_own = dk_own + dk_more[:, lanes]
                    dv_own = dv_own + dv_more[:, lanes]
                right[rows_of(i), pl.ds(pl.multiple_of(QKV + feat + hp * half, half), half)] = dk_own.astype(BF16)
                right[rows_of(i), pl.ds(pl.multiple_of(QKV + 2 * feat + hp * half, half), half)] = dv_own.astype(BF16)
            if i == 0:
                step(EARLY[1] + first_pair, 0)
            return carry

        lax.fori_loop(0, feat // half // pairs, group, 0)
        right[rows_of(i), QKV : QKV + feat] = dqt[...].T
        d_normed = None
        for j in range(3):
            term = dot_nt(
                right[rows_of(i), QKV + j * feat : QKV + (j + 1) * feat], wqkv[:, j * feat : (j + 1) * feat]
            )
            d_normed = term if d_normed is None else d_normed + term
        return d_mixed + norm_back(state[i], d_normed, row(gain1_ref), 0, i == 1)

    wait_inputs(0)
    arrivals[1].wait()
    send_inputs(1)
    state[0] = x_ref[...].astype(F32)
    first = forward(0)
    state[1] = first.astype(BF16).astype(F32) + row(embed_ref)
    second = forward(1)
    out_seq[...] = (second * inside).astype(BF16)
    wait_inputs(1)

    def send_results(n):
        @pl.when(p > 0)
        def _():
            for j in range(1, size):
                result_copies(j)[n].start()
            own_results()[n].start()

    send_results(0)
    d_carry = backward(1, cot_ref[...].astype(F32) * inside)
    vec_part[4:5, :] = jnp.sum(d_carry, axis=0, keepdims=True)
    vec_part[5:8, :] = jnp.zeros((3, feat), F32)
    d_state = backward(0, d_carry.astype(BF16).astype(F32))
    grad_seq[...] = d_state.astype(BF16)

    begun = EARLY[1] + feat // half // BACKWARD_PAIRS[0]
    vector_step(0)

    def late_step(t, carry):
        step(t, 0)
        for i in range(1, len(ways) + 1):
            @pl.when(t == begun + 3 * i)
            def _(i=i):
                vector_step(i)

        @pl.when(t == chunks + offsets[1])
        def _():
            send_results(1)

        return carry

    lax.fori_loop(begun, chunks + offsets[-1], late_step, 0)
    vec_ref[...] = vec_sum[len(ways)]

    @pl.when(p > 0)
    def _():
        for copy in own_results():
            copy.wait()
        for j in range(1, size):
            for copy in result_copies(j):
                copy.wait_send()

    for j in range(1, size):
        source = (p + size - j) % size

        @pl.when(source > 0)
        def _(j=j, source=source):
            for n, dst in enumerate((out_ref, gin_ref)):
                pltpu.make_async_copy(dst.at[source - 1], dst.at[source - 1], o_rs.at[n, j - 1]).wait()

    for h in range(2):
        pltpu.make_async_copy(full.at[:, h], full.at[:, h], s_sem.at[h]).wait()


def run_block(inputs, cotangent, lengths, vectors, w_qkv, w_out, w_up, w_down, rows, lags, groups):
    slots, block, feat = inputs.shape
    ff = w_up.shape[1]
    seq = (slots + 1) * block
    quarter = feat // 4
    units = (2 * ff + 4 * feat) // feat
    chunks = units * (quarter // rows)
    piece = rows // ZED
    half = feat // 2
    ways = 5 + (groups > 1)
    landings = 5 + (groups - 1)
    more = max(groups - 1, 1)
    dma = pltpu.SemaphoreType.DMA
    local_block = jax.ShapeDtypeStruct((slots, block, feat), BF16)
    left_rows = ff + 3 * feat
    right_cols = 5 * feat + ff
    return pl.pallas_call(
        functools.partial(block_kernel, (rows, lags, groups)),
        out_shape=(
            jax.ShapeDtypeStruct((quarter, units * feat), BF16),
            local_block,
            local_block,
            jax.ShapeDtypeStruct((8, feat), F32),
        ),
        in_specs=[ANY, ANY, SMEM] + [VMEM] * 5 + [ANY] * 4,
        out_specs=(ANY, VMEM, VMEM, VMEM),
        scratch_shapes=[
            pltpu.VMEM(inputs.shape, BF16),
            pltpu.VMEM(inputs.shape, BF16),
            pltpu.VMEM((seq, feat), BF16),
            pltpu.VMEM((seq, feat), BF16),
            pltpu.VMEM((seq, feat), BF16),
            pltpu.VMEM((seq, feat), BF16),
            pltpu.VMEM((8, feat), F32),
            pltpu.VMEM((ways + 1, 8, feat), F32),
            pltpu.VMEM(w_qkv.shape, BF16),
            pltpu.VMEM(w_out.shape, BF16),
            pltpu.VMEM(w_up.shape, BF16),
            pltpu.VMEM(w_down.shape, BF16),
            pltpu.VMEM((left_rows, 2 * seq), BF16),
            pltpu.VMEM((2 * seq, right_cols), BF16),
            pltpu.VMEM((2, seq, 3 * feat), BF16),
            pltpu.VMEM((2, feat, seq), BF16),
            pltpu.VMEM((2, feat, seq), BF16),
            pltpu.VMEM((2, 16, seq), F32),
            pltpu.VMEM((2, seq, ff), BF16),
            pltpu.VMEM((2, seq, feat), F32),
            pltpu.VMEM((2, seq, feat), F32),
            pltpu.VMEM((seq, feat), BF16),
            pltpu.VMEM((seq, feat), F32),
            pltpu.VMEM((seq, feat), F32),
            pltpu.VMEM((feat, seq), BF16),
            pltpu.VMEM((seq, feat), BF16),
            pltpu.VMEM((seq, seq), F32),
            pltpu.VMEM((2, 2, rows, feat), F32),
            pltpu.VMEM((2, 2, rows, feat), BF16),
            pltpu.VMEM((SLOTS, 2, rows, feat), BF16),
            pltpu.VMEM((SLOTS, rows, feat), BF16),
            pltpu.VMEM((SLOTS, rows, feat), F32),
            pltpu.VMEM((SLOTS, rows, feat), BF16),
            pltpu.VMEM((SLOTS, rows, half), BF16),
            pltpu.VMEM((SLOTS, rows, half), F32),
            pltpu.VMEM((SLOTS, rows, half), BF16),
            pltpu.VMEM((SLOTS, rows, half), BF16),
            pltpu.VMEM((SLOTS, ZED - 1, piece, half), BF16),
            pltpu.VMEM((SLOTS if groups > 1 else 1, piece, half), BF16),
            pltpu.VMEM((SLOTS if groups > 1 else 1, more, piece, half), BF16),
            pltpu.VMEM((chunks, 2, rows, half), BF16),
            pltpu.VMEM((landings, 8, feat), F32),
            dma((2,)), dma((4,)), dma((2, slots)), dma((2, slots)),
            dma((SLOTS,)), dma((SLOTS,)), dma((SLOTS,)), dma((SLOTS,)), dma((SLOTS,)), dma((SLOTS,)),
            dma((SLOTS, ZED - 1)), dma((SLOTS, ZED - 1)),
            dma((SLOTS if groups > 1 else 1, more)), dma((SLOTS if groups > 1 else 1, more)),
            dma((SLOTS, ZED - 1)), dma((SLOTS, ZED - 1)),
            dma((SLOTS,)), dma((SLOTS,)), dma((2,)),
            dma((2, slots)), dma((2, slots)), dma((landings,)), dma((landings,)), dma((2,)),
        ],
        compiler_params=pltpu.CompilerParams(
            collective_id=0, has_side_effects=True, vmem_limit_bytes=60 * 2**20
        ),
    )(inputs, cotangent, lengths, *vectors, w_qkv, w_out, w_up, w_down)


def finish_kernel(
    sums_hbm, block_ref, grads_ref, vec_ref,
    block_out, grads_out, qkv_out, out_out, up_out, down_out, gain1_out, shift1_out, gain2_out, shift2_out, embed_out,
    low, high, l_sem, s_sem, c_sem,
):
    feat = vec_ref.shape[1]
    quarter = feat // 4
    units, tiles = low.shape[0], up_out.shape[1] // feat
    passed = [
        pltpu.make_async_copy(block_ref, block_out, c_sem.at[0]),
        pltpu.make_async_copy(grads_ref, grads_out, c_sem.at[1]),
    ]
    loads = [
        pltpu.make_async_copy(sums_hbm.at[:, pl.ds(u * feat, feat)], low.at[u], l_sem.at[u]) for u in range(units)
    ]
    for copy in loads + passed:
        copy.start()
    vec = pltpu.roll(vec_ref[...], feat - quarter * lax.axis_index("pipe"), 1)
    for n, ref in enumerate((gain1_out, shift1_out, gain2_out, shift2_out, embed_out)):
        ref[...] = vec[n, :quarter]
    stores = []
    for u in range(units):
        loads[u].wait()
        high[u] = low[u].astype(F32)
        if u < tiles:
            place = down_out.at[pl.ds(u * quarter, quarter)]
        elif u < 2 * tiles:
            place = up_out.at[:, pl.ds((u - tiles) * feat, feat)]
        elif u == 2 * tiles:
            place = out_out
        else:
            place = qkv_out.at[:, pl.ds((u - 2 * tiles - 1) * feat, feat)]
        copy = pltpu.make_async_copy(high.at[u], place, s_sem.at[u])
        copy.start()
        stores.append(copy)
    for copy in stores + passed:
        copy.wait()


def run_finish(sums, block_out, input_grads, vec, ff):
    feat = vec.shape[1]
    quarter = feat // 4
    units = sums.shape[1] // feat
    dma = pltpu.SemaphoreType.DMA

    def result(*shape):
        return jax.ShapeDtypeStruct(shape, F32)

    return pl.pallas_call(
        finish_kernel,
        out_shape=(
            jax.ShapeDtypeStruct(block_out.shape, BF16),
            jax.ShapeDtypeStruct(input_grads.shape, BF16),
            result(quarter, 3 * feat), result(quarter, feat), result(quarter, ff), result(ff // 4, feat),
        ) + (result(quarter),) * 5,
        in_specs=[ANY, VMEM, VMEM, VMEM],
        out_specs=(ANY,) * 6 + (VMEM,) * 5,
        scratch_shapes=[
            pltpu.VMEM((units, quarter, feat), BF16),
            pltpu.VMEM((units, quarter, feat), F32),
            dma((units,)), dma((units,)), dma((2,)),
        ],
        compiler_params=pltpu.CompilerParams(vmem_limit_bytes=60 * 2**20),
    )(sums, block_out, input_grads, vec)


def shards(
    inputs, lengths, w_qkv, w_out, w_up, w_down, norm1_gain, norm1_shift, norm2_gain, norm2_shift, pass_embed, cotangent
):
    ff = w_up.shape[1]
    groups = lax.axis_size("dp") // (2 * ZED)
    vectors = (norm1_gain, norm1_shift, norm2_gain, norm2_shift, pass_embed)
    sums, block_out, input_grads, vec = run_block(
        inputs, cotangent, lengths, vectors, w_qkv, w_out, w_up, w_down, ROWS, LAGS[: 7 + (groups > 1)], groups
    )
    return run_finish(sums, block_out, input_grads, vec, ff)


def solution(mesh):
    rep = P()
    seqs = P("dp", "pipe", None)
    return jax.shard_map(
        shards,
        mesh=mesh,
        in_specs=(seqs, P("dp")) + (rep,) * 9 + (seqs,),
        out_specs=(seqs, seqs) + (P("pipe", None),) * 4 + (P("pipe"),) * 5,
        check_vma=False,
    )
```

```python
import functools

import jax
import jax.numpy as jnp
from jax import lax
from jax.experimental import pallas as pl
from jax.experimental.pallas import tpu as pltpu
from jax.sharding import PartitionSpec as P

MESH = pl.DeviceIdType.MESH
HEADS = 12
HEAD = 64
F32 = jnp.float32
BF16 = jnp.bfloat16
ANY = pl.BlockSpec(memory_space=pl.ANY)
VMEM = pl.BlockSpec(memory_space=pltpu.VMEM)
SMEM = pl.BlockSpec(memory_space=pltpu.SMEM)


def dot(left, right):
    return jnp.dot(left, right, preferred_element_type=F32)


def dot_nt(left, right):
    return lax.dot_general(left, right, (((1,), (1,)), ((), ())), preferred_element_type=F32)


def row(ref):
    return ref[...].reshape(1, ref.shape[0])


def normalize(values):
    center = values - jnp.mean(values, axis=-1, keepdims=True)
    scale = lax.rsqrt(jnp.mean(center * center, axis=-1, keepdims=True) + 1e-05)
    return center * scale, scale


ZED = 4
SLOTS = 8
ROWS = 64
LAGS = (0, 1, 2, 2, 2, 2, 2, 2, 2)
EARLY = (3, 6)
EARLY_CHUNKS = 12
FORWARD_PAIRS = 6
BACKWARD_PAIRS = (1, 6)


def block_kernel(
    dims, in_hbm, given_hbm, len_ref, gain1_ref, shift1_ref, gain2_ref, shift2_ref, embed_ref,
    wqkv_hbm, wout_hbm, wup_hbm, wdown_hbm,
    sums_hbm, out_ref, gin_ref, vec_ref,
    in_ref, given_ref, x_ref, cot_ref, out_seq, grad_seq, vec_part, vec_sum,
    wqkv, wout, wup, wdown, left, right, qkv, vt, kt, lse, gp, mixed, state, ctx,
    dk_more, dv_more, dqt, dctx, bias,
    own, give, d_recv, y_send, y_keep, y_recv, x_send, x_keep, x_recv,
    z_send, z_recv, w_send, w_recv, full, vec_recv,
    a_sem, w_sem, i_ss, i_rs, d_ss, d_rs, y_ss, y_rs, x_ss, x_rs, z_ss, z_rs, w_ss, w_rs, g_ss, g_rs, h_ss, h_rs, s_sem,
    o_ss, o_rs, v_ss, v_rs, local,
):
    rows, lags, groups = dims
    slots, block, feat = in_hbm.shape
    size = slots + 1
    seq = size * block
    ff = wup.shape[1]
    tiles = ff // feat
    half = feat // 6
    units = (2 * ff + 4 * feat) // feat
    quarter = feat // 4
    subs = quarter // rows
    chunks = units * subs
    piece = rows // ZED
    g = lax.axis_index("dp")
    p = lax.axis_index("pipe")
    core, y = p % 2, p // 2
    x, z, w = g % 2, (g // 2) % ZED, g // (2 * ZED)
    sib = (g, p + 1 - 2 * core)
    ypeer = (g, p + 2 - 4 * y)
    diag = (g, 3 - p)
    xpeer = (g + 1 - 2 * x, p)

    def zpeer(j):
        return (g + 2 * ((z + j) % ZED - z), p)

    def wpeer(j):
        return (g + 2 * ZED * ((w + j) % groups - w), p)

    def zflip(step):
        return (2 * ZED * w + 2 * (z + step * (1 - 2 * ((z // step) % 2))) + x, p)

    everyone = [sib, ypeer, diag, xpeer] + [zpeer(j) for j in range(1, ZED)] + [wpeer(j) for j in range(1, groups)]

    arrivals = [
        pltpu.make_async_copy(in_hbm, in_ref, a_sem.at[0]),
        pltpu.make_async_copy(given_hbm, given_ref, a_sem.at[1]),
    ]
    for copy in arrivals:
        copy.start()
    weight_copies = [
        pltpu.make_async_copy(src, dst, w_sem.at[i])
        for i, (src, dst) in enumerate(
            ((wqkv_hbm, wqkv), (wout_hbm, wout), (wup_hbm, wup), (wdown_hbm, wdown))
        )
    ]
    for copy in weight_copies:
        copy.start()

    barrier = pltpu.get_barrier_semaphore()
    for device in everyone:
        pl.semaphore_signal(barrier, inc=1, device_id=device, device_id_type=MESH)
    pl.semaphore_wait(barrier, len(everyone))

    mine = pl.ds(pl.multiple_of(p * block, block), block)

    def input_copies(j):
        peer = (p + j) % size
        slot = jnp.maximum(peer - 1, 0)
        return [
            pltpu.make_async_remote_copy(
                src.at[slot], dst.at[mine], i_ss.at[n, j - 1], i_rs.at[n, j - 1],
                device_id=(g, peer), device_id_type=MESH,
            )
            for n, (src, dst) in enumerate(((in_ref, x_ref), (given_ref, cot_ref)))
        ]

    def own_inputs():
        slot = jnp.maximum(p - 1, 0)
        return [
            pltpu.make_async_copy(src.at[slot], dst.at[mine], local.at[n])
            for n, (src, dst) in enumerate(((in_ref, x_ref), (given_ref, cot_ref)))
        ]

    def wait_inputs(n):
        @pl.when(p > 0)
        def _():
            own_inputs()[n].wait()
            for j in range(1, size):
                input_copies(j)[n].wait_recv()

        for j in range(1, size):
            @pl.when((p + j) % size > 0)
            def _(j=j):
                input_copies(j)[n].wait_send()

    def send_inputs(n):
        for j in range(1, size):
            @pl.when((p + j) % size > 0)
            def _(j=j):
                input_copies(j)[n].start()

        @pl.when(p > 0)
        def _():
            own_inputs()[n].start()

    arrivals[0].wait()
    send_inputs(0)

    @pl.when(p == 0)
    def _():
        x_ref[...] = jnp.zeros(x_ref.shape, x_ref.dtype)
        cot_ref[...] = jnp.zeros(cot_ref.shape, cot_ref.dtype)

    slots, block, _ = out_ref.shape
    size = slots + 1

    def result_copies(j):
        peer = (p + j) % size
        slot = jnp.maximum(p - 1, 0)
        part = pl.ds(pl.multiple_of(peer * block, block), block)
        return [
            pltpu.make_async_remote_copy(
                src.at[part], dst.at[slot], o_ss.at[n, j - 1], o_rs.at[n, j - 1],
                device_id=(g, peer), device_id_type=MESH,
            )
            for n, (src, dst) in enumerate(((out_seq, out_ref), (grad_seq, gin_ref)))
        ]

    def own_results():
        part = pl.ds(pl.multiple_of(p * block, block), block)
        slot = jnp.maximum(p - 1, 0)
        return [
            pltpu.make_async_copy(out_seq.at[part], out_ref.at[slot], local.at[0]),
            pltpu.make_async_copy(grad_seq.at[part], gin_ref.at[slot], local.at[1]),
        ]

    def copy_d(c):
        return pltpu.make_async_remote_copy(
            give.at[c % 2], d_recv.at[c % SLOTS], d_ss.at[c % SLOTS], d_rs.at[c % SLOTS], device_id=sib, device_id_type=MESH
        )

    def copy_y(c):
        return pltpu.make_async_remote_copy(
            y_send.at[c % SLOTS], y_recv.at[c % SLOTS], y_ss.at[c % SLOTS], y_rs.at[c % SLOTS], device_id=ypeer, device_id_type=MESH
        )

    def copy_x(c):
        return pltpu.make_async_remote_copy(
            x_send.at[c % SLOTS, 0], x_recv.at[c % SLOTS, 0], x_ss.at[c % SLOTS], x_rs.at[c % SLOTS], device_id=xpeer, device_id_type=MESH
        )

    def early_copy_x(c):
        return pltpu.make_async_remote_copy(
            x_send.at[c % SLOTS], x_recv.at[c % SLOTS], x_ss.at[c % SLOTS], x_rs.at[c % SLOTS],
            device_id=xpeer, device_id_type=MESH,
        )

    def early_copy_y(c):
        cols = pl.ds(0, feat // 2)
        return pltpu.make_async_remote_copy(
            y_send.at[c % SLOTS, :, cols], y_recv.at[c % SLOTS, :, cols], y_ss.at[c % SLOTS], y_rs.at[c % SLOTS],
            device_id=ypeer, device_id_type=MESH,
        )

    def part_of(k):
        return pl.ds(pl.multiple_of(k * piece, piece), piece)

    def copy_z(c, j):
        return pltpu.make_async_remote_copy(
            z_send.at[c % SLOTS, part_of((z + j) % ZED)], z_recv.at[c % SLOTS, j - 1], z_ss.at[c % SLOTS, j - 1], z_rs.at[c % SLOTS, j - 1],
            device_id=zpeer(j), device_id_type=MESH,
        )

    def copy_w(c, j):
        return pltpu.make_async_remote_copy(
            w_send.at[c % SLOTS], w_recv.at[c % SLOTS, j - 1], w_ss.at[c % SLOTS, j - 1], w_rs.at[c % SLOTS, j - 1],
            device_id=wpeer(j), device_id_type=MESH,
        )

    def copy_g(c, n):
        other = z + 2 - 4 * (z // 2)
        place = full.at[c, x, part_of(other if n == 2 else z)]
        return pltpu.make_async_remote_copy(
            place, place, g_ss.at[c % SLOTS, n], g_rs.at[c % SLOTS, n],
            device_id=zflip(2 if n == 0 else 1), device_id_type=MESH,
        )

    def copy_h(c):
        place = full.at[c, x]
        return pltpu.make_async_remote_copy(
            place, place, h_ss.at[c % SLOTS], h_rs.at[c % SLOTS], device_id=xpeer, device_id_type=MESH
        )

    def copy_s(c):
        u, s = c // subs, c % subs
        half = feat // 2
        return [
            pltpu.make_async_copy(
                full.at[c, h],
                sums_hbm.at[
                    pl.ds(pl.multiple_of(s * rows, rows), rows),
                    pl.ds(pl.multiple_of(u * feat + h * half, half), half),
                ],
                s_sem.at[h],
            )
            for h in range(2)
        ]

    def make(c):
        u, s = c // subs, c % subs

        def left_rows(q):
            down = feat * q + quarter * u
            rest = ff + feat * ((u >= 2 * tiles).astype(jnp.int32) + (u > 2 * tiles).astype(jnp.int32)) + quarter * q
            start = jnp.where(u < tiles, down, rest) + s * rows
            return left[pl.ds(pl.multiple_of(start, rows), rows), :]

        order = (2 * (1 - y) + core, 2 * y + core, 2 * (1 - y) + 1 - core, 2 * y + 1 - core)
        lhs = jnp.concatenate([left_rows(q) for q in order], axis=0)
        cols = pl.ds(pl.multiple_of(feat * jnp.maximum(u - tiles + 1, 0), feat), feat)
        total = jnp.dot(lhs, right[:, cols], preferred_element_type=F32)
        slot = c % 2
        own[slot, 0] = total[:rows]
        own[slot, 1] = total[rows : 2 * rows]
        give[slot, 0] = total[2 * rows : 3 * rows].astype(BF16)
        give[slot, 1] = total[3 * rows :].astype(BF16)
        copy_d(c).start()

    def stage_y(c):
        copy_d(c).wait()
        slot = c % 2
        y_send[c % SLOTS] = (own[slot, 0] + d_recv[c % SLOTS, 0].astype(F32)).astype(BF16)
        copy_y(c).start()
        y_keep[c % SLOTS] = own[slot, 1] + d_recv[c % SLOTS, 1].astype(F32)

    def stage_x(c):
        copy_y(c).wait()
        half = feat // 2
        total = y_keep[c % SLOTS] + y_recv[c % SLOTS].astype(F32)

        @pl.when(x == 0)
        def _():
            x_send[c % SLOTS, 0] = total[:, half:].astype(BF16)
            x_keep[c % SLOTS, 0] = total[:, :half]

        @pl.when(x == 1)
        def _():
            x_send[c % SLOTS, 0] = total[:, :half].astype(BF16)
            x_keep[c % SLOTS, 0] = total[:, half:]

        copy_x(c).start()

    def stage_z(c):
        copy_x(c).wait()
        send_z(c, x_keep[c % SLOTS, 0] + x_recv[c % SLOTS, 0].astype(F32))

    def early_x(c):
        copy_d(c).wait()
        half = feat // 2
        sums = [own[c % 2, n] + d_recv[c % SLOTS, n].astype(F32) for n in range(2)]
        for side in range(2):
            @pl.when(x == side)
            def _(side=side):
                for n in range(2):
                    x_send[c % SLOTS, n] = sums[n][:, (1 - side) * half : (2 - side) * half].astype(BF16)
                    x_keep[c % SLOTS, n] = sums[n][:, side * half : (side + 1) * half]

        early_copy_x(c).start()

    def early_y(c):
        early_copy_x(c).wait()
        y_send[c % SLOTS, :, : feat // 2] = (x_keep[c % SLOTS, 0] + x_recv[c % SLOTS, 0].astype(F32)).astype(BF16)
        early_copy_y(c).start()
        x_keep[c % SLOTS, 1] += x_recv[c % SLOTS, 1].astype(F32)

    def early_z(c):
        early_copy_y(c).wait()
        send_z(c, x_keep[c % SLOTS, 1] + y_recv[c % SLOTS, :, : feat // 2].astype(F32))

    def send_z(c, total):
        z_send[c % SLOTS] = total.astype(BF16)
        for j in range(1, ZED):
            copy_z(c, j).start()

    def add_z(c):
        for j in range(1, ZED):
            copy_z(c, j).wait()
        total = z_send[c % SLOTS, part_of(z)].astype(F32)
        for j in range(1, ZED):
            total = total + z_recv[c % SLOTS, j - 1].astype(F32)
        return total

    def stage_w(c):
        w_send[c % SLOTS] = add_z(c).astype(BF16)
        for j in range(1, groups):
            copy_w(c, j).start()

    def add_w(c):
        for j in range(1, groups):
            copy_w(c, j).wait()
        total = w_send[c % SLOTS].astype(F32)
        for j in range(1, groups):
            total = total + w_recv[c % SLOTS, j - 1].astype(F32)
        return total

    def stage_g(c):
        full[c, x, part_of(z)] = (add_z(c) if groups == 1 else add_w(c)).astype(BF16)
        copy_g(c, 0).start()
        copy_g(c, 1).start()

    def stage_g2(c):
        copy_g(c, 0).wait()
        copy_g(c, 2).start()

    def stage_h(c):
        copy_g(c, 1).wait()
        copy_g(c, 2).wait()
        copy_h(c).start()

    def stage_s(c):
        copy_h(c).wait()
        for copy in copy_s(c):
            copy.start()

    ways = [[sib], [ypeer], [xpeer], [zflip(1)], [zflip(2)]]
    if groups > 1:
        ways.append([wpeer(j) for j in range(1, groups)])
    firsts = [sum(len(way) for way in ways[:i]) for i in range(len(ways))]

    def vector_copies(i):
        return [
            pltpu.make_async_remote_copy(
                vec_sum.at[i], vec_recv.at[firsts[i] + n], v_ss.at[firsts[i] + n], v_rs.at[firsts[i] + n],
                device_id=device, device_id_type=MESH,
            )
            for n, device in enumerate(ways[i])
        ]

    def vector_step(i):
        if i == 0:
            vec_sum[0] = vec_part[...]
        else:
            for copy in vector_copies(i - 1):
                copy.wait()
            total = vec_sum[i - 1]
            for n in range(len(ways[i - 1])):
                total = total + vec_recv[firsts[i - 1] + n]
            vec_sum[i] = total
        if i < len(ways):
            for copy in vector_copies(i):
                copy.start()

    stages = [make, stage_y, stage_x, stage_z] + ([stage_w] if groups > 1 else []) + [stage_g, stage_g2, stage_h, stage_s]
    offsets = [sum(lags[: i + 1]) for i in range(len(stages))]
    early_stages = {1: early_x, 2: early_y, 3: early_z}

    def step(t, carry):
        for i, (stage, offset) in enumerate(zip(stages, offsets)):
            c = t - offset
            present = (c >= 0) & (c < chunks)
            if i in early_stages:
                early = (c < EARLY_CHUNKS) & (c % 2 == 1)

                @pl.when(present & early)
                def _(stage=early_stages[i], c=c):
                    stage(c)

                present = present & ((c >= EARLY_CHUNKS) | (c % 2 == 0))

            @pl.when(present)
            def _(stage=stage, c=c):
                stage(c)

        return carry

    def run_steps(first, end):
        lax.fori_loop(first, end, step, 0)

    length = len_ref[jnp.maximum(p - 1, 0)]
    keys = lax.broadcasted_iota(jnp.int32, (seq, seq), 0)
    queries = lax.broadcasted_iota(jnp.int32, (seq, seq), 1)
    bias[...] = jnp.where((keys <= queries) & (keys < length), 0.0, -1e30).astype(F32)
    inside = (lax.broadcasted_iota(jnp.int32, (seq, 1), 0) < length).astype(F32)
    low_lanes = lax.broadcasted_iota(jnp.int32, (seq, half), 1) < HEAD

    def pick(values, head):
        zero = jnp.zeros_like(values)
        return jnp.where(low_lanes, values, zero) if head == 0 else jnp.where(low_lanes, zero, values)

    def rows_of(i):
        return pl.ds(i * seq, seq)

    def put_left(offset, i, values):
        left[pl.ds(offset, values.shape[1]), rows_of(i)] = values.T

    N2, CTX, N1 = ff, ff + feat, ff + 2 * feat
    HID, ATT, QKV = feat, feat + ff, 2 * feat + ff

    def forward(i):
        value = state[i]
        n1 = (normalize(value)[0] * row(gain1_ref) + row(shift1_ref)).astype(BF16)
        put_left(N1, i, n1)
        if i == 0:
            weight_copies[0].wait()
        for j in range(3):
            part = dot(n1, wqkv[:, j * feat : (j + 1) * feat])
            if j == 0:
                part = part * HEAD ** (-0.5)
            part = part.astype(BF16)
            qkv[i, :, j * feat : (j + 1) * feat] = part
            if j == 1:
                kt[i] = part.T
            if j == 2:
                vt[i] = part.T

        def group(first_pair, carry):
            mid = seq // 2
            heads = [(u, head) for u in range(FORWARD_PAIRS) for head in range(2)]
            scores = []
            for u, head in heads:
                hp = first_pair * FORWARD_PAIRS + u
                qm = pick(qkv[i, :, pl.ds(pl.multiple_of(hp * half, half), half)], head)
                scores.append([
                    dot_nt(qkv[b, :, pl.ds(pl.multiple_of(feat + hp * half, half), half)], qm)
                    for b in range(i + 1)
                ])
            weights, invs = [], []
            for n, (u, head) in enumerate(heads):
                hp = first_pair * FORWARD_PAIRS + u
                low = [s[:mid, :mid] + bias[:mid, :mid] for s in scores[n]]
                high = [s[:, mid:] + bias[:, mid:] for s in scores[n]]
                parts = []
                stats = []
                for blocks in (low, high):
                    top = functools.reduce(jnp.maximum, [jnp.max(s, axis=0, keepdims=True) for s in blocks])
                    w = [jnp.exp(s - top) for s in blocks]
                    total = sum(jnp.sum(v, axis=0, keepdims=True) for v in w)
                    parts.append([v.astype(BF16) for v in w])
                    stats.append((top, total))
                top = jnp.concatenate([stats[0][0], stats[1][0]], axis=1)
                total = jnp.concatenate([stats[0][1], stats[1][1]], axis=1)
                lse[i, pl.ds(2 * hp + head, 1), :] = top + jnp.log(total)
                zero = jnp.zeros((mid, mid), BF16)
                weights.append([
                    jnp.concatenate([jnp.concatenate([lo, zero], axis=0), hi], axis=1) for lo, hi in zip(*parts)
                ])
                invs.append(1.0 / total)
            for n, (u, head) in enumerate(heads):
                hp = first_pair * FORWARD_PAIRS + u
                rows = pl.ds(pl.multiple_of(hp * half + head * HEAD, HEAD), HEAD)
                acc = sum(dot(vt[b, rows, :], weights[n][b]) for b in range(i + 1)) * invs[n]
                left[pl.ds(pl.multiple_of(CTX + hp * half + head * HEAD, HEAD), HEAD), rows_of(i)] = acc.astype(BF16)
            return carry

        lax.fori_loop(0, feat // half // FORWARD_PAIRS, group, 0)
        ctx[...] = left[pl.ds(CTX, feat), rows_of(i)].T
        if i == 0:
            weight_copies[1].wait()
        mix = state[i] + dot(ctx[...], wout[...])
        mixed[i] = mix
        n2 = (normalize(mix)[0] * row(gain2_ref) + row(shift2_ref)).astype(BF16)
        put_left(N2, i, n2)
        if i == 0:
            weight_copies[2].wait()
            weight_copies[3].wait()
        acc = mix
        for j in range(tiles):
            u = dot(n2, wup[:, j * feat : (j + 1) * feat])
            c = 0.7978845608028654
            square = u * u
            th = jnp.tanh(c * u * (1.0 + 0.044715 * square))
            halfp = 0.5 + 0.5 * th
            active = (u * halfp).astype(BF16)
            slope = halfp + 0.5 * u * (1.0 - th * th) * (c * (1.0 + 3 * 0.044715 * square))
            gp[i, :, j * feat : (j + 1) * feat] = slope.astype(BF16)
            put_left(j * feat, i, active)
            acc = acc + dot(active, wdown[j * feat : (j + 1) * feat, :])
        return acc

    def norm_back(values, d_out, gain, slot, first):
        norm, scale = normalize(values)
        g_gain = jnp.sum(d_out * norm, axis=0, keepdims=True)
        g_shift = jnp.sum(d_out, axis=0, keepdims=True)
        if first:
            vec_part[slot : slot + 1, :] = g_gain
            vec_part[slot + 1 : slot + 2, :] = g_shift
        else:
            vec_part[slot : slot + 1, :] += g_gain
            vec_part[slot + 1 : slot + 2, :] += g_shift
        t = d_out * gain
        return scale * (t - jnp.mean(t, axis=-1, keepdims=True) - norm * jnp.mean(t * norm, axis=-1, keepdims=True))

    def backward(i, grad):
        pairs = BACKWARD_PAIRS[i]
        branch = grad.astype(BF16)
        right[rows_of(i), 0:feat] = branch
        if i == 0:
            run_steps(0, EARLY[0])
        acc = None
        for j in range(tiles):
            d_active = dot_nt(branch, wdown[j * feat : (j + 1) * feat, :])
            d_hidden = (d_active * gp[i, :, j * feat : (j + 1) * feat].astype(F32)).astype(BF16)
            right[rows_of(i), HID + j * feat : HID + (j + 1) * feat] = d_hidden
            term = dot_nt(d_hidden, wup[:, j * feat : (j + 1) * feat])
            acc = term if acc is None else acc + term
        if i == 0:
            run_steps(EARLY[0], EARLY[1])
        d_mixed = grad + norm_back(mixed[i], acc, row(gain2_ref), 2, i == 1)
        d_attn = d_mixed.astype(BF16)
        right[rows_of(i), ATT : ATT + feat] = d_attn
        dctx[...] = dot_nt(d_attn, wout[...]).astype(BF16)

        def group(first_pair, carry):
            mid = seq // 2
            for u in range(pairs):
                hp = first_pair * pairs + u
                lanes = pl.ds(pl.multiple_of(hp * half, half), half)
                q2 = qkv[i, :, lanes]
                do2 = dctx[:, lanes]
                dk = [None] * (i + 1)
                dv = [None] * (i + 1)
                zero = jnp.zeros((mid, mid), BF16)
                for head in range(2):
                    qm = pick(q2, head)
                    dom = pick(do2, head)
                    lrow = lse[i, pl.ds(2 * hp + head, 1), :]
                    soft = [[], []]
                    d_soft = [[], []]
                    for b in range(i + 1):
                        k2 = qkv[b, :, pl.ds(pl.multiple_of(feat + hp * half, half), half)]
                        v2 = qkv[b, :, pl.ds(pl.multiple_of(2 * feat + hp * half, half), half)]
                        s = dot_nt(k2, qm)
                        d = dot_nt(v2, dom)
                        soft[0].append(jnp.exp(s[:mid, :mid] + (bias[:mid, :mid] - lrow[:, :mid])))
                        soft[1].append(jnp.exp(s[:, mid:] + (bias[:, mid:] - lrow[:, mid:])))
                        d_soft[0].append(d[:mid, :mid])
                        d_soft[1].append(d[:, mid:])
                    inner = [
                        sum(jnp.sum(a * c, axis=0, keepdims=True) for a, c in zip(soft[h], d_soft[h])) for h in range(2)
                    ]
                    rows = pl.ds(pl.multiple_of(hp * half + head * HEAD, HEAD), HEAD)
                    dq = None

                    def whole(lo, hi):
                        return jnp.concatenate([jnp.concatenate([lo, zero], axis=0), hi], axis=1)

                    for b in range(i + 1):
                        d_score = whole(*[(soft[h][b] * (d_soft[h][b] - inner[h])).astype(BF16) for h in range(2)])
                        prob = whole(*[soft[h][b].astype(BF16) for h in range(2)])
                        term_v = dot(prob, dom)
                        term_k = dot(d_score, qm)
                        term_q = dot(kt[b, rows, :], d_score)
                        dv[b] = term_v if dv[b] is None else dv[b] + term_v
                        dk[b] = term_k if dk[b] is None else dk[b] + term_k
                        dq = term_q if dq is None else dq + term_q
                    dqt[rows, :] = (dq * HEAD ** (-0.5)).astype(BF16)
                dk_own, dv_own = dk[i], dv[i]
                if i == 1:
                    dk_more[:, lanes] = dk[0]
                    dv_more[:, lanes] = dv[0]
                else:
                    dk_own = dk_own + dk_more[:, lanes]
                    dv_own = dv_own + dv_more[:, lanes]
                right[rows_of(i), pl.ds(pl.multiple_of(QKV + feat + hp * half, half), half)] = dk_own.astype(BF16)
                right[rows_of(i), pl.ds(pl.multiple_of(QKV + 2 * feat + hp * half, half), half)] = dv_own.astype(BF16)
            if i == 0:
                step(EARLY[1] + first_pair, 0)
            return carry

        lax.fori_loop(0, feat // half // pairs, group, 0)
        right[rows_of(i), QKV : QKV + feat] = dqt[...].T
        d_normed = None
        for j in range(3):
            term = dot_nt(
                right[rows_of(i), QKV + j * feat : QKV + (j + 1) * feat], wqkv[:, j * feat : (j + 1) * feat]
            )
            d_normed = term if d_normed is None else d_normed + term
        return d_mixed + norm_back(state[i], d_normed, row(gain1_ref), 0, i == 1)

    wait_inputs(0)
    arrivals[1].wait()
    send_inputs(1)
    state[0] = x_ref[...].astype(F32)
    first = forward(0)
    state[1] = first.astype(BF16).astype(F32) + row(embed_ref)
    second = forward(1)
    out_seq[...] = (second * inside).astype(BF16)
    wait_inputs(1)

    def send_results(n):
        @pl.when(p > 0)
        def _():
            for j in range(1, size):
                result_copies(j)[n].start()
            own_results()[n].start()

    send_results(0)
    d_carry = backward(1, cot_ref[...].astype(F32) * inside)
    vec_part[4:5, :] = jnp.sum(d_carry, axis=0, keepdims=True)
    vec_part[5:8, :] = jnp.zeros((3, feat), F32)
    d_state = backward(0, d_carry.astype(BF16).astype(F32))
    grad_seq[...] = d_state.astype(BF16)

    begun = EARLY[1] + feat // half // BACKWARD_PAIRS[0]
    vector_step(0)

    def late_step(t, carry):
        step(t, 0)
        for i in range(1, len(ways) + 1):
            @pl.when(t == begun + 3 * i)
            def _(i=i):
                vector_step(i)

        @pl.when(t == chunks + offsets[1])
        def _():
            send_results(1)

        return carry

    lax.fori_loop(begun, chunks + offsets[-1], late_step, 0)
    vec_ref[...] = vec_sum[len(ways)]

    @pl.when(p > 0)
    def _():
        for copy in own_results():
            copy.wait()
        for j in range(1, size):
            for copy in result_copies(j):
                copy.wait_send()

    for j in range(1, size):
        source = (p + size - j) % size

        @pl.when(source > 0)
        def _(j=j, source=source):
            for n, dst in enumerate((out_ref, gin_ref)):
                pltpu.make_async_copy(dst.at[source - 1], dst.at[source - 1], o_rs.at[n, j - 1]).wait()

    for h in range(2):
        pltpu.make_async_copy(full.at[:, h], full.at[:, h], s_sem.at[h]).wait()


def run_block(inputs, cotangent, lengths, vectors, w_qkv, w_out, w_up, w_down, rows, lags, groups):
    slots, block, feat = inputs.shape
    ff = w_up.shape[1]
    seq = (slots + 1) * block
    quarter = feat // 4
    units = (2 * ff + 4 * feat) // feat
    chunks = units * (quarter // rows)
    piece = rows // ZED
    half = feat // 2
    ways = 5 + (groups > 1)
    landings = 5 + (groups - 1)
    more = max(groups - 1, 1)
    dma = pltpu.SemaphoreType.DMA
    local_block = jax.ShapeDtypeStruct((slots, block, feat), BF16)
    left_rows = ff + 3 * feat
    right_cols = 5 * feat + ff
    return pl.pallas_call(
        functools.partial(block_kernel, (rows, lags, groups)),
        out_shape=(
            jax.ShapeDtypeStruct((quarter, units * feat), BF16),
            local_block,
            local_block,
            jax.ShapeDtypeStruct((8, feat), F32),
        ),
        in_specs=[ANY, ANY, SMEM] + [VMEM] * 5 + [ANY] * 4,
        out_specs=(ANY, VMEM, VMEM, VMEM),
        scratch_shapes=[
            pltpu.VMEM(inputs.shape, BF16),
            pltpu.VMEM(inputs.shape, BF16),
            pltpu.VMEM((seq, feat), BF16),
            pltpu.VMEM((seq, feat), BF16),
            pltpu.VMEM((seq, feat), BF16),
            pltpu.VMEM((seq, feat), BF16),
            pltpu.VMEM((8, feat), F32),
            pltpu.VMEM((ways + 1, 8, feat), F32),
            pltpu.VMEM(w_qkv.shape, BF16),
            pltpu.VMEM(w_out.shape, BF16),
            pltpu.VMEM(w_up.shape, BF16),
            pltpu.VMEM(w_down.shape, BF16),
            pltpu.VMEM((left_rows, 2 * seq), BF16),
            pltpu.VMEM((2 * seq, right_cols), BF16),
            pltpu.VMEM((2, seq, 3 * feat), BF16),
            pltpu.VMEM((2, feat, seq), BF16),
            pltpu.VMEM((2, feat, seq), BF16),
            pltpu.VMEM((2, 16, seq), F32),
            pltpu.VMEM((2, seq, ff), BF16),
            pltpu.VMEM((2, seq, feat), F32),
            pltpu.VMEM((2, seq, feat), F32),
            pltpu.VMEM((seq, feat), BF16),
            pltpu.VMEM((seq, feat), F32),
            pltpu.VMEM((seq, feat), F32),
            pltpu.VMEM((feat, seq), BF16),
            pltpu.VMEM((seq, feat), BF16),
            pltpu.VMEM((seq, seq), F32),
            pltpu.VMEM((2, 2, rows, feat), F32),
            pltpu.VMEM((2, 2, rows, feat), BF16),
            pltpu.VMEM((SLOTS, 2, rows, feat), BF16),
            pltpu.VMEM((SLOTS, rows, feat), BF16),
            pltpu.VMEM((SLOTS, rows, feat), F32),
            pltpu.VMEM((SLOTS, rows, feat), BF16),
            pltpu.VMEM((SLOTS, 2, rows, half), BF16),
            pltpu.VMEM((SLOTS, 2, rows, half), F32),
            pltpu.VMEM((SLOTS, 2, rows, half), BF16),
            pltpu.VMEM((SLOTS, rows, half), BF16),
            pltpu.VMEM((SLOTS, ZED - 1, piece, half), BF16),
            pltpu.VMEM((SLOTS if groups > 1 else 1, piece, half), BF16),
            pltpu.VMEM((SLOTS if groups > 1 else 1, more, piece, half), BF16),
            pltpu.VMEM((chunks, 2, rows, half), BF16),
            pltpu.VMEM((landings, 8, feat), F32),
            dma((2,)), dma((4,)), dma((2, slots)), dma((2, slots)),
            dma((SLOTS,)), dma((SLOTS,)), dma((SLOTS,)), dma((SLOTS,)), dma((SLOTS,)), dma((SLOTS,)),
            dma((SLOTS, ZED - 1)), dma((SLOTS, ZED - 1)),
            dma((SLOTS if groups > 1 else 1, more)), dma((SLOTS if groups > 1 else 1, more)),
            dma((SLOTS, ZED - 1)), dma((SLOTS, ZED - 1)),
            dma((SLOTS,)), dma((SLOTS,)), dma((2,)),
            dma((2, slots)), dma((2, slots)), dma((landings,)), dma((landings,)), dma((2,)),
        ],
        compiler_params=pltpu.CompilerParams(
            collective_id=0, has_side_effects=True, vmem_limit_bytes=61 * 2**20
        ),
    )(inputs, cotangent, lengths, *vectors, w_qkv, w_out, w_up, w_down)


def finish_kernel(
    sums_hbm, block_ref, grads_ref, vec_ref,
    block_out, grads_out, qkv_out, out_out, up_out, down_out, gain1_out, shift1_out, gain2_out, shift2_out, embed_out,
    low, high, l_sem, s_sem, c_sem,
):
    feat = vec_ref.shape[1]
    quarter = feat // 4
    units, tiles = low.shape[0], up_out.shape[1] // feat
    passed = [
        pltpu.make_async_copy(block_ref, block_out, c_sem.at[0]),
        pltpu.make_async_copy(grads_ref, grads_out, c_sem.at[1]),
    ]
    loads = [
        pltpu.make_async_copy(sums_hbm.at[:, pl.ds(u * feat, feat)], low.at[u], l_sem.at[u]) for u in range(units)
    ]
    for copy in loads + passed:
        copy.start()
    vec = pltpu.roll(vec_ref[...], feat - quarter * lax.axis_index("pipe"), 1)
    for n, ref in enumerate((gain1_out, shift1_out, gain2_out, shift2_out, embed_out)):
        ref[...] = vec[n, :quarter]
    stores = []
    for u in range(units):
        loads[u].wait()
        high[u] = low[u].astype(F32)
        if u < tiles:
            place = down_out.at[pl.ds(u * quarter, quarter)]
        elif u < 2 * tiles:
            place = up_out.at[:, pl.ds((u - tiles) * feat, feat)]
        elif u == 2 * tiles:
            place = out_out
        else:
            place = qkv_out.at[:, pl.ds((u - 2 * tiles - 1) * feat, feat)]
        copy = pltpu.make_async_copy(high.at[u], place, s_sem.at[u])
        copy.start()
        stores.append(copy)
    for copy in stores + passed:
        copy.wait()


def run_finish(sums, block_out, input_grads, vec, ff):
    feat = vec.shape[1]
    quarter = feat // 4
    units = sums.shape[1] // feat
    dma = pltpu.SemaphoreType.DMA

    def result(*shape):
        return jax.ShapeDtypeStruct(shape, F32)

    return pl.pallas_call(
        finish_kernel,
        out_shape=(
            jax.ShapeDtypeStruct(block_out.shape, BF16),
            jax.ShapeDtypeStruct(input_grads.shape, BF16),
            result(quarter, 3 * feat), result(quarter, feat), result(quarter, ff), result(ff // 4, feat),
        ) + (result(quarter),) * 5,
        in_specs=[ANY, VMEM, VMEM, VMEM],
        out_specs=(ANY,) * 6 + (VMEM,) * 5,
        scratch_shapes=[
            pltpu.VMEM((units, quarter, feat), BF16),
            pltpu.VMEM((units, quarter, feat), F32),
            dma((units,)), dma((units,)), dma((2,)),
        ],
        compiler_params=pltpu.CompilerParams(vmem_limit_bytes=60 * 2**20),
    )(sums, block_out, input_grads, vec)


def shards(
    inputs, lengths, w_qkv, w_out, w_up, w_down, norm1_gain, norm1_shift, norm2_gain, norm2_shift, pass_embed, cotangent
):
    ff = w_up.shape[1]
    groups = lax.axis_size("dp") // (2 * ZED)
    vectors = (norm1_gain, norm1_shift, norm2_gain, norm2_shift, pass_embed)
    sums, block_out, input_grads, vec = run_block(
        inputs, cotangent, lengths, vectors, w_qkv, w_out, w_up, w_down, ROWS, LAGS[: 8 + (groups > 1)], groups
    )
    return run_finish(sums, block_out, input_grads, vec, ff)


def solution(mesh):
    rep = P()
    seqs = P("dp", "pipe", None)
    return jax.shard_map(
        shards,
        mesh=mesh,
        in_specs=(seqs, P("dp")) + (rep,) * 9 + (seqs,),
        out_specs=(seqs, seqs) + (P("pipe", None),) * 4 + (P("pipe"),) * 5,
        check_vma=False,
    )
```
